512 devices in a mesh: bins: 128 (over z_lo, y, x), ch: 4 (over z_hi, core).
Axes of the slice: x: 4, y: 4, z: 16 (z_hi: 2, z_lo: 8; z = z_hi * 8 + z_lo), core: 2. Of those that a mesh axis runs over, the one named last changes fastest.
Arguments:
- inputs: bfloat16 [65536, 768], P('bins', 'ch'), may hold values from -6 to 6
- cotangent: bfloat16 [65536, 768], P('bins', 'ch'), may hold values from -6 to 6
- first_kernel_weight: bfloat16 [3, 768, 768], P(None, 'ch'), may hold values from -0.125 to 0.125
- second_kernel_weight: bfloat16 [3, 768, 768], P(None, 'ch'), may hold values from -0.125 to 0.125
Outputs:
- activations: bfloat16 [65536, 768], P('bins', 'ch')
- input_grad: bfloat16 [65536, 768], P('bins', 'ch')
- grad_near: bfloat16 [3, 768, 768], P(None, 'ch')
- grad_far: bfloat16 [3, 768, 768], P(None, 'ch')
The draws below stay inside these ranges and needn't reach their ends.
All inputs are finite; a program needn't handle non-finite values.
Results may differ from the reference program's by a relative error of at most 0.013.
Values may be sent and summed in bfloat16 or wider, within the bound.
A program may use at most 64 MiB of HBM per device.

```python
import math
import jax
import jax.numpy as jnp

C = 768
DILATION_FIRST = 512
DILATION_SECOND = 2048
BINS = 65536


def shard_levels(key, dims, shards, low, largest):
    def one(dim, blocks):
        heights = jax.random.uniform(jax.random.fold_in(jax.random.fold_in(key, 6), dim), (blocks,), jnp.float32, low / len(shards), largest / len(shards))
        return jnp.repeat(jnp.exp(heights), dims[dim] // blocks).reshape((-1,) + (1,) * (len(dims) - dim - 1))

    factor_of = one(*shards[0])
    for cut in shards[1:]:
        factor_of = factor_of * one(*cut)
    return factor_of


def scatter_about(rng, extent, scale, most, split=(), kind=jnp.bfloat16):
    drawn = scale * jax.random.normal(rng, extent, jnp.float32)
    if split:
        drawn = drawn * shard_levels(rng, extent, split, -0.22, 0.18)
    return jnp.clip(drawn, -most, most).astype(kind)


def setup_inputs(seed: int = 0) -> dict:
    key_list = jax.random.split(jax.random.key(seed), 5)
    inputs = scatter_about(key_list[0], (BINS, C), 1.0, 6.0, ((0, 128), (1, 4)))
    cotangent = scatter_about(key_list[1], (BINS, C), 1.0, 6.0, ((0, 128), (1, 4)))
    first_kernel_weight = scatter_about(key_list[2], (3, C, C), (3 * C) ** -0.5, 0.125, ((1, 4),))
    second_kernel_weight = scatter_about(key_list[3], (3, C, C), (3 * C) ** -0.5, 0.125, ((1, 4),))
    return {"inputs": inputs, "cotangent": cotangent, "first_kernel_weight": first_kernel_weight, "second_kernel_weight": second_kernel_weight}


gelu_coeff = 0.7978845608

def gelu_value(values):
    inner = gelu_coeff * (values + 0.044715 * values * values * values)
    return 0.5 * values * (1.0 + jnp.tanh(inner))

def gelu_slope(values):
    inner = gelu_coeff * (values + 0.044715 * values * values * values)
    tangent = jnp.tanh(inner)
    return 0.5 * (1.0 + tangent) + 0.5 * values * (1.0 - tangent * tangent) * gelu_coeff * (1.0 + 3.0 * 0.044715 * values * values)

def offset_rows(values, shift_by):
    if shift_by == 0:
        return values
    padding = jnp.zeros((abs(shift_by), values.shape[1]), values.dtype)
    if shift_by > 0:
        return jnp.concatenate([values[shift_by:], padding], axis=0)
    return jnp.concatenate([padding, values[:shift_by]], axis=0)

def reference(inputs, cotangent, first_kernel_weight, second_kernel_weight):
    residual_blocks = ((first_kernel_weight, DILATION_FIRST), (second_kernel_weight, DILATION_SECOND))
    current = inputs
    stored = []
    for weight, dilation in residual_blocks:
        activated = gelu_value(current.astype(jnp.float32)).astype(jnp.bfloat16)
        conv_out = jnp.zeros(current.shape, jnp.float32)
        for tap_index in range(3):
            moved = offset_rows(activated, (tap_index - 1) * dilation)
            conv_out = conv_out + jnp.dot(moved, weight[tap_index], preferred_element_type=jnp.float32)
        stored.append((current, activated))
        current = (current.astype(jnp.float32) + conv_out).astype(jnp.bfloat16)
    norm_scale = 1.0 / math.sqrt(BINS)
    gradient = cotangent
    kernel_grads = [None, None]
    for block_number in (1, 0):
        weight, dilation = residual_blocks[block_number]
        previous, activated = stored[block_number]
        back_sum = jnp.zeros(previous.shape, jnp.float32)
        sequence_parts = []
        for tap_index in range(3):
            moved_grad = offset_rows(gradient, -(tap_index - 1) * dilation)
            back_sum = back_sum + jnp.dot(moved_grad, weight[tap_index].T, preferred_element_type=jnp.float32)
            moved = offset_rows(activated, (tap_index - 1) * dilation)
            sequence_parts.append(jnp.dot(moved.T, gradient, preferred_element_type=jnp.float32))
        kernel_grads[block_number] = (jnp.stack(sequence_parts) * norm_scale).astype(jnp.bfloat16)
        gradient = (gradient.astype(jnp.float32) + gelu_slope(previous.astype(jnp.float32)) * back_sum).astype(jnp.bfloat16)
    return (current, gradient, kernel_grads[0], kernel_grads[1])
```

```python
import math

import jax
import jax.numpy as jnp
from jax import lax
from jax.experimental import pallas as pl
from jax.experimental.pallas import tpu as pltpu
from jax.sharding import PartitionSpec as P

DILATION_FIRST = 512
DILATION_SECOND = 2048
MESH = pl.DeviceIdType.MESH
NUM_X, NUM_Y, NUM_Z = 4, 4, 8
UNITS = 27


gelu_coeff = 0.7978845608


def passed_along(block, axis, distance):
    devices = range(lax.axis_size(axis))
    route = [(i - distance, i) for i in devices if i - distance in devices]
    return lax.ppermute(block, axis, route)


def gelu_value(values):
    inner = gelu_coeff * (values + 0.044715 * values * values * values)
    return 0.5 * values * (1.0 + jnp.tanh(inner))


def gelu_slope(values):
    inner = gelu_coeff * (values + 0.044715 * values * values * values)
    tangent = jnp.tanh(inner)
    return 0.5 * (1.0 + tangent) + 0.5 * values * (1.0 - tangent * tangent) * gelu_coeff * (
        1.0 + 3.0 * 0.044715 * values * values
    )


def against_kernel(full_grad, kernel):
    return lax.dot_general(
        full_grad, kernel, (((1,), (1,)), ((), ())), preferred_element_type=jnp.float32
    )


def over_rows(left_rows, right_rows):
    return lax.dot_general(
        left_rows, right_rows, (((0,), (0,)), ((), ())), preferred_element_type=jnp.float32
    )


def device_hops(dilation, bin_rows):
    return max(dilation // bin_rows, 1)


class Place:
    def __init__(self):
        b = lax.axis_index("bins")
        self.b = b
        self.ch = lax.axis_index("ch")
        self.x = lax.rem(b, 4)
        self.y = lax.rem(lax.div(b, 4), 4)
        self.z = lax.div(b, 16)

    def shifted(self, axis, d):
        x, y, z = self.x, self.y, self.z
        if axis == "x":
            x = lax.rem(x + d, 4)
        elif axis == "y":
            y = lax.rem(y + d, 4)
        else:
            z = lax.rem(z + d, 8)
        return (z * 16 + y * 4 + x, self.ch)

    def coordinate(self, axis):
        return {"x": self.x, "y": self.y, "z": self.z}[axis]


AXES = (("x", "y"), ("y", "x"))


def unit_place(linear):
    tap, rest = divmod(linear, 72)
    row, col = divmod(rest, 6)
    return tap, row * 16, col * 128


def send(src, dst, send_sem, recv_sem, target):
    copy = pltpu.make_async_remote_copy(
        src_ref=src,
        dst_ref=dst,
        send_sem=send_sem,
        recv_sem=recv_sem,
        device_id=target,
        device_id_type=MESH,
    )
    copy.start()
    return copy


def sum_kernel(near_ref, far_ref, near_out, far_out, d1, r1, d2, r2, d3, r3, g3, g2, g1,
               s1, q1, s2, q2, s3, q3, s4, q4, s5, q5, s6, q6):
    me = Place()
    barrier = pltpu.get_barrier_semaphore()
    for axis, n in (("x", 4), ("y", 4), ("z", 8)):
        for d in range(1, n):
            pl.semaphore_signal(barrier, inc=1, device_id=me.shifted(axis, d), device_id_type=MESH)
    sent = []
    parts = [(b, p) for b in (1, 0) for p in (0, 1)]
    sources = (near_ref, far_ref)
    results = (near_out, far_out)
    for b, p in parts:
        for q in range(4):
            for r in range(UNITS):
                tap, row, col = unit_place(p * 108 + q * UNITS + r)
                d1[2 * b + p, q, r] = sources[b][tap, row : row + 16, col : col + 128].astype(jnp.bfloat16)
    pl.semaphore_wait(barrier, 13)

    first = {}
    for b, p in parts:
        i = 2 * b + p
        axis = AXES[p][0]
        here = me.coordinate(axis)
        for d in (1, 2, 3):
            first[i, d] = send(d1.at[i, lax.rem(here + d, 4)], r1.at[i, d - 1], s1.at[i, d - 1], q1.at[i, d - 1],
                               me.shifted(axis, d))
    second = {}
    for b, p in parts:
        i = 2 * b + p
        here = me.coordinate(AXES[p][0])
        for d in (1, 2, 3):
            first[i, d].wait_recv()
        for r in range(0, UNITS, 9):
            total = d1[i, here, r : r + 9].astype(jnp.float32)
            for d in range(3):
                total = total + r1[i, d, r : r + 9].astype(jnp.float32)
            d2[i, r : r + 9] = total.astype(jnp.bfloat16)
        d2[i, UNITS:] = jnp.zeros((32 - UNITS, 16, 128), jnp.bfloat16)
        axis = AXES[p][1]
        there = me.coordinate(axis)
        for d in (1, 2, 3):
            second[i, d] = send(d2.at[i, pl.ds(lax.rem(there + d, 4) * 8, 8)], r2.at[i, d - 1], s2.at[i, d - 1],
                                q2.at[i, d - 1], me.shifted(axis, d))
    third = {}
    for b, p in parts:
        i = 2 * b + p
        there = me.coordinate(AXES[p][1])
        for d in (1, 2, 3):
            second[i, d].wait_recv()
        total = d2[i, pl.ds(there * 8, 8)].astype(jnp.float32)
        for d in range(3):
            total = total + r2[i, d].astype(jnp.float32)
        d3[i] = total.astype(jnp.bfloat16)
        for d in range(1, 8):
            third[i, d] = send(d3.at[i, lax.rem(me.z + d, 8)], r3.at[i, d - 1], s3.at[i, d - 1], q3.at[i, d - 1],
                               me.shifted("z", d))
    fourth = {}
    scale = 1.0 / math.sqrt(65536)
    for b, p in parts:
        i = 2 * b + p
        for d in range(1, 8):
            third[i, d].wait_recv()
        total = d3[i, me.z].astype(jnp.float32)
        for d in range(7):
            total = total + r3[i, d].astype(jnp.float32)
        g3[i, me.z] = (total * scale).astype(jnp.bfloat16)
        for d in range(1, 8):
            fourth[i, d] = send(g3.at[i, me.z], g3.at[i, me.z], s4.at[i, d - 1], q4.at[i, d - 1],
                                me.shifted("z", d))
    fifth = {}
    for b, p in parts:
        i = 2 * b + p
        axis = AXES[p][1]
        there = me.coordinate(axis)
        for d in range(1, 8):
            fourth[i, d].wait_recv()
        for d in (1, 2, 3):
            fifth[i, d] = send(g3.at[i], g2.at[i, pl.ds(there * 8, 8)], s5.at[i, d - 1], q5.at[i, d - 1],
                               me.shifted(axis, d))
        g2[i, pl.ds(there * 8, 8)] = g3[i]
    sixth = {}
    for b, p in parts:
        i = 2 * b + p
        axis = AXES[p][0]
        here = me.coordinate(axis)
        for d in (1, 2, 3):
            fifth[i, d].wait_recv()
        for d in (1, 2, 3):
            sixth[i, d] = send(g2.at[i, pl.ds(0, UNITS)], g1.at[i, here], s6.at[i, d - 1], q6.at[i, d - 1],
                               me.shifted(axis, d))
        g1[i, here] = g2[i, :UNITS]
    for b, p in parts:
        i = 2 * b + p
        for d in (1, 2, 3):
            sixth[i, d].wait_recv()
        for q in range(4):
            for r in range(UNITS):
                tap, row, col = unit_place(p * 108 + q * UNITS + r)
                results[b][tap, row : row + 16, col : col + 128] = g1[i, q, r]
    for group in (first, second, third, fourth, fifth, sixth):
        for copy in group.values():
            copy.wait_send()


def summed(near, far):
    out = jax.ShapeDtypeStruct((3, 192, 768), jnp.bfloat16)
    vmem = pl.BlockSpec(memory_space=pltpu.VMEM)

    def buffer(*lead):
        return pltpu.VMEM((4,) + lead + (16, 128), jnp.bfloat16)

    def sems(n):
        return [pltpu.SemaphoreType.DMA((4, n))] * 2

    return pl.pallas_call(
        sum_kernel,
        out_shape=(out, out),
        in_specs=[vmem] * 2,
        out_specs=(vmem, vmem),
        scratch_shapes=[
            buffer(4, UNITS), buffer(3, UNITS), buffer(32), buffer(3, 8), buffer(8), buffer(7),
            buffer(8), buffer(32), buffer(4, UNITS),
        ] + sems(3) + sems(3) + sems(7) + sems(7) + sems(3) + sems(3),
        compiler_params=pltpu.CompilerParams(
            collective_id=0, has_side_effects=True, vmem_limit_bytes=48 * 2**20
        ),
    )(near, far)


def body(inputs, cotangent, first_kernel_weight, second_kernel_weight):
    bin_rows = inputs.shape[0]
    residual_blocks = (
        (first_kernel_weight, DILATION_FIRST),
        (second_kernel_weight, DILATION_SECOND),
    )
    current = inputs
    stored = []
    for weight, dilation in residual_blocks:
        hop_count = device_hops(dilation, bin_rows)
        activated = gelu_value(current.astype(jnp.float32)).astype(jnp.bfloat16)
        got_earlier = passed_along(activated, "bins", hop_count)
        got_later = passed_along(activated, "bins", -hop_count)
        tap_rows = (got_earlier, activated, got_later)
        partial_value = jnp.dot(got_earlier, weight[0], preferred_element_type=jnp.float32)
        partial_value = partial_value + jnp.dot(
            activated, weight[1], preferred_element_type=jnp.float32
        )
        partial_value = partial_value + jnp.dot(
            got_later, weight[2], preferred_element_type=jnp.float32
        )
        conv_out = lax.psum_scatter(partial_value, "ch", scatter_dimension=1, tiled=True)
        stored.append((current, tap_rows))
        current = (current.astype(jnp.float32) + conv_out).astype(jnp.bfloat16)
    gradient = cotangent
    local_grads = [None, None]
    for block_number in (1, 0):
        weight, dilation = residual_blocks[block_number]
        hop_count = device_hops(dilation, bin_rows)
        previous, tap_rows = stored[block_number]
        full_grad = lax.all_gather(gradient, "ch", axis=1, tiled=True)
        got_later = passed_along(full_grad, "bins", -hop_count)
        got_earlier = passed_along(full_grad, "bins", hop_count)
        back_sum = against_kernel(got_later, weight[0])
        back_sum = back_sum + against_kernel(full_grad, weight[1])
        back_sum = back_sum + against_kernel(got_earlier, weight[2])
        local_kernel = jnp.stack(
            [
                over_rows(tap_rows[0], full_grad),
                over_rows(tap_rows[1], full_grad),
                over_rows(tap_rows[2], full_grad),
            ]
        )
        local_grads[block_number] = local_kernel
        gradient = (
            gradient.astype(jnp.float32) + gelu_slope(previous.astype(jnp.float32)) * back_sum
        ).astype(jnp.bfloat16)
    grad_near, grad_far = summed(local_grads[0], local_grads[1])
    return (current, gradient, grad_near, grad_far)


def solution(mesh):
    return jax.shard_map(
        body,
        mesh=mesh,
        in_specs=(P("bins", "ch"), P("bins", "ch"), P(None, "ch", None), P(None, "ch", None)),
        out_specs=(P("bins", "ch"), P("bins", "ch"), P(None, "ch", None), P(None, "ch", None)),
        check_vma=False,
    )
```

```python
import math

import jax
import jax.numpy as jnp
from jax import lax
from jax.experimental import pallas as pl
from jax.experimental.pallas import tpu as pltpu
from jax.sharding import PartitionSpec as P

MESH = pl.DeviceIdType.MESH
ROWS = 512
CHUNKS = 4
CHUNK = ROWS // CHUNKS
UNITS = 27
LAST_BIN = 127
BINS = 65536
F32, BF16 = jnp.float32, jnp.bfloat16

gelu_coeff = 0.7978845608

AXES = (("x", "y"), ("y", "x"))


def gelu_value(values):
    inner = gelu_coeff * (values + 0.044715 * values * values * values)
    return 0.5 * values * (1.0 + jnp.tanh(inner))


def gelu_slope(values):
    inner = gelu_coeff * (values + 0.044715 * values * values * values)
    tangent = jnp.tanh(inner)
    return 0.5 * (1.0 + tangent) + 0.5 * values * (1.0 - tangent * tangent) * gelu_coeff * (
        1.0 + 3.0 * 0.044715 * values * values
    )


def product(left, right):
    return jnp.dot(left, right, preferred_element_type=F32)


def against(left, right):
    return lax.dot_general(left, right, (((1,), (1,)), ((), ())), preferred_element_type=F32)


def over_rows(left, right):
    return lax.dot_general(left, right, (((0,), (0,)), ((), ())), preferred_element_type=F32)


class Place:
    def __init__(self):
        b = lax.axis_index("bins")
        self.b = b
        self.ch = lax.axis_index("ch")
        self.half = lax.div(self.ch, 2)
        self.core = lax.rem(self.ch, 2)
        self.x = lax.rem(b, 4)
        self.y = lax.rem(lax.div(b, 4), 4)
        self.z = lax.div(b, 16)
        self.other_half = (b, lax.rem(self.ch + 2, 4))
        self.other_core = (b, self.half * 2 + 1 - self.core)

    def shifted(self, axis, d):
        x, y, z = self.x, self.y, self.z
        if axis == "x":
            x = lax.rem(x + d, 4)
        elif axis == "y":
            y = lax.rem(y + d, 4)
        else:
            z = lax.rem(z + d, 8)
        return (z * 16 + y * 4 + x, self.ch)

    def along(self, distance):
        return (lax.rem(self.b + distance + 128, 128), self.ch)

    def coordinate(self, axis):
        return {"x": self.x, "y": self.y, "z": self.z}[axis]


def remote(src, dst, send_sem, recv_sem, target):
    return pltpu.make_async_remote_copy(
        src_ref=src,
        dst_ref=dst,
        send_sem=send_sem,
        recv_sem=recv_sem,
        device_id=target,
        device_id_type=MESH,
    )


class Sender:
    def __init__(self):
        self.pending = []

    def __call__(self, src, dst, sems, index, target):
        copy = remote(src, dst, sems[0].at[index], sems[1].at[index], target)
        copy.start()
        self.pending.append((None, copy))
        return copy

    def when(self, condition, src, dst, sems, index, target):
        copy = remote(src, dst, sems[0].at[index], sems[1].at[index], target)

        @pl.when(condition)
        def _():
            copy.start()

        self.pending.append((condition, copy))
        return copy

    def finish(self):
        for condition, copy in self.pending:
            if condition is None:
                copy.wait_send()
            else:
                pl.when(condition)(copy.wait_send)


def kernel(x_ref, c_ref, w1_ref, w2_ref, act_out, grad_out, near_out, far_out, *scratch):
    s = dict(zip(SCRATCH, scratch))
    me = Place()
    half, core = me.half, me.core
    send = Sender()
    barrier = pltpu.get_barrier_semaphore()

    def sems(name):
        return s[name + "_s"], s[name + "_r"]

    def neighbours(hops):
        return me.b >= hops, me.b <= LAST_BIN - hops

    near_low, near_high = neighbours(1)
    far_low, far_high = neighbours(4)

    for axis, n in (("x", 4), ("y", 4), ("z", 8)):
        for d in range(1, n):
            pl.semaphore_signal(barrier, inc=1, device_id=me.shifted(axis, d), device_id_type=MESH)
    pl.semaphore_signal(barrier, inc=1, device_id=me.other_half, device_id_type=MESH)
    pl.semaphore_signal(barrier, inc=1, device_id=me.other_core, device_id_type=MESH)
    for hops, condition in ((-1, near_low), (1, near_high), (-4, far_low), (4, far_high)):

        @pl.when(condition)
        def _(hops=hops):
            pl.semaphore_signal(barrier, inc=1, device_id=me.along(hops), device_id_type=MESH)

    x0p, u1, x1p, u2, g2, g1 = (s[n] for n in ("x0p", "u1", "x1p", "u2", "g2", "g1"))

    def blank(condition, ref):
        @pl.when(jnp.logical_not(condition))
        def _():
            ref[...] = jnp.zeros(ref.shape, ref.dtype)

    blank(near_low, u1.at[0])
    blank(near_high, u1.at[2])
    blank(far_low, u2.at[0])
    blank(far_high, u2.at[2])

    @pl.when(jnp.logical_not(far_high))
    def _():
        g2[0, core] = jnp.zeros((ROWS, 384), BF16)

    @pl.when(jnp.logical_not(far_low))
    def _():
        g2[2, core] = jnp.zeros((ROWS, 384), BF16)

    @pl.when(jnp.logical_not(near_high))
    def _():
        g1[0, core] = jnp.zeros((ROWS, 384), BF16)

    @pl.when(jnp.logical_not(near_low))
    def _():
        g1[2, core] = jnp.zeros((ROWS, 384), BF16)

    def pack(ref, packed, main_at, tail_at):
        for m in range(CHUNKS):
            top = m * CHUNK
            packed[m, :CHUNK] = ref[top : top + CHUNK, main_at : main_at + 128]
            upper = ref[top : top + 64, tail_at : tail_at + 64]
            lower = ref[top + 64 : top + 128, tail_at : tail_at + 64]
            packed[m, CHUNK:] = jnp.concatenate([upper, lower], axis=1)

    @pl.when(core == 0)
    def _():
        pack(x_ref, s["xs"], 0, 128)
        pack(c_ref, s["cs"], 0, 128)

    @pl.when(core == 1)
    def _():
        pack(x_ref, s["xs"], 64, 0)
        pack(c_ref, s["cs"], 64, 0)

    wires = 15 + sum(c.astype(jnp.int32) for c in (near_low, near_high, far_low, far_high))
    pl.semaphore_wait(barrier, wires)

    weights = (w1_ref, w2_ref)
    parts = [(b, p) for b in (0, 1) for p in (0, 1)]

    wh, we, wf = s["wh"], s["we"], s["wf"]
    crossing = {}
    for b, p in parts:
        i = 2 * b + p
        first, second = me.coordinate(AXES[p][0]), me.coordinate(AXES[p][1])
        place = lax.rem(second * 8 + me.z, UNITS)
        unit = p * 108 + first * UNITS + place
        tap = lax.div(unit, 72)
        rest = lax.rem(unit, 72)
        row = pl.multiple_of(lax.div(rest, 6) * 16, 16)
        col = pl.multiple_of(lax.rem(rest, 6) * 128, 128)
        crossing[i] = send(
            weights[b].at[tap, pl.ds(row, 16), pl.ds(col, 128)], s["wu"].at[i], sems("wx"), i, me.other_half
        )
    xcopy = [send(s["xs"].at[m], s["xr"].at[m], sems("xx"), m, me.other_half) for m in range(CHUNKS)]
    ccopy = [send(s["cs"].at[m], s["cr"].at[m], sems("cx"), m, me.other_half) for m in range(CHUNKS)]

    def gather_lines(i, grouped, name):
        return [
            send(grouped.at[i, me.z], grouped.at[i, me.z], sems(name), (i, d - 1), me.shifted("z", d))
            for d in range(1, 8)
        ]

    def gather_second(i, p, grouped, wide, name):
        axis = AXES[p][1]
        there = pl.ds(me.coordinate(axis) * 8, 8)
        copies = [
            send(grouped.at[i], wide.at[i, there], sems(name), (i, d - 1), me.shifted(axis, d)) for d in (1, 2, 3)
        ]
        wide[i, there] = grouped[i]
        return copies

    def gather_first(b, p, wide, whole, name):
        axis = AXES[p][0]
        i = 2 * b + p
        here = pl.ds(p * 108 + me.coordinate(axis) * UNITS, UNITS)
        copies = [
            send(wide.at[i, pl.ds(0, UNITS)], whole.at[b, here], sems(name), (i, d - 1), me.shifted(axis, d))
            for d in (1, 2, 3)
        ]
        whole[b, here] = wide[i, :UNITS]
        return copies

    def arrived(copies):
        for copy in copies:
            copy.wait_recv()

    def paired(mine, theirs):
        own = mine[CHUNK:].astype(F32)
        other = theirs[CHUNK:].astype(F32)
        low = jnp.where(half == 0, own, other)
        high = jnp.where(half == 0, other, own)
        upper = jnp.concatenate([low[:, :64], high[:, :64]], axis=1)
        lower = jnp.concatenate([low[:, 64:], high[:, 64:]], axis=1)
        own_main = mine[:CHUNK].astype(F32)
        other_main = theirs[:CHUNK].astype(F32)
        return (
            jnp.where(half == 0, own_main, other_main),
            jnp.where(half == 0, other_main, own_main),
            jnp.concatenate([upper, lower], axis=0),
        )

    near_copies = []
    far_u_copies = []

    def x_chunk(m):
        xcopy[m].wait_recv()
        rows = pl.ds(m * CHUNK, CHUNK)
        for t, tile in enumerate(paired(s["xs"].at[m], s["xr"].at[m])):
            x0p[rows, t * 128 : (t + 1) * 128] = tile.astype(BF16)
            u1[1, rows, t * 128 : (t + 1) * 128] = gelu_value(tile).astype(BF16)
        low = send.when(near_low, u1.at[1, rows], u1.at[2, rows], sems("u1h"), (0, m), me.along(-1))
        high = send.when(near_high, u1.at[1, rows], u1.at[0, rows], sems("u1h"), (1, m), me.along(1))
        near_copies.append((near_high, low))
        near_copies.append((near_low, high))

    g2_copies, g2_core = [], []

    def c_chunk(m):
        ccopy[m].wait_recv()
        rows = pl.ds(m * CHUNK, CHUNK)
        for t, tile in enumerate(paired(s["cs"].at[m], s["cr"].at[m])):
            g2[1, core, rows, t * 128 : (t + 1) * 128] = tile.astype(BF16)
        mine = g2.at[1, core, rows]
        low = send.when(far_low, mine, g2.at[0, core, rows], sems("g2h"), (0, m), me.along(-4))
        high = send.when(far_high, mine, g2.at[2, core, rows], sems("g2h"), (1, m), me.along(4))
        g2_copies.append((far_high, low))
        g2_copies.append((far_low, high))
        g2_core.append(send(mine, g2.at[1, core, rows], sems("g2c"), m, me.other_core))

    def halo_arrived(copies):
        for condition, copy in copies:
            pl.when(condition)(copy.wait_recv)

    x_chunk(0)
    lines, seconds, firsts = {}, {}, {}
    for b, p in parts:
        i = 2 * b + p
        crossing[i].wait_recv()
        wh[i, me.z] = s["wu"][i]
        lines[i] = gather_lines(i, wh, "wz")
    x_chunk(1)
    for b, p in parts:
        i = 2 * b + p
        arrived(lines[i])
        seconds[i] = gather_second(i, p, wh, we, "w2")
    x_chunk(2)
    for b, p in parts:
        i = 2 * b + p
        arrived(seconds[i])
        firsts[i] = gather_first(b, p, we, wf, "w1")
    x_chunk(3)
    c_chunk(0)

    def assemble(b, out):
        ref = weights[b]
        own_main, own_tail = half * 128, 256 + half * 64
        other_main, other_tail = 128 - half * 128, 320 - half * 64

        def columns(tiles):
            low, high = tiles[1], tiles[4]
            return (
                tiles[0],
                tiles[3],
                jnp.concatenate([low[:, :64], high[:, :64]], axis=1),
                tiles[2],
                tiles[5],
                jnp.concatenate([low[:, 64:], high[:, 64:]], axis=1),
            )

        def step(k, _):
            tap, i = lax.div(k, 12), lax.rem(k, 12)
            natural = lax.rem(i + 4 * core, 12)
            tail = i >= 8
            own_at = jnp.where(tail, own_tail + (i - 8) * 16, own_main + i * 16)
            other_at = jnp.where(tail, other_tail + (i - 8) * 16, other_main + i * 16)
            own_at, other_at = pl.multiple_of(own_at, 16), pl.multiple_of(other_at, 16)
            rows = pl.ds(pl.multiple_of(natural * 16, 16), 16)
            own = columns([ref[tap, rows, t * 128 : (t + 1) * 128] for t in range(6)])
            other = columns([wf[b, tap * 72 + natural * 6 + t] for t in range(6)])
            for t in range(6):
                out[tap, pl.ds(own_at, 16), t * 128 : (t + 1) * 128] = own[t]
                out[tap, pl.ds(other_at, 16), t * 128 : (t + 1) * 128] = other[t]
            return 0

        lax.fori_loop(0, 36, step, 0)

    arrived(firsts[0])
    arrived(firsts[1])
    assemble(0, s["wp1"])
    c_chunk(1)
    halo_arrived(near_copies)

    wp1, wp2 = s["wp1"], s["wp2"]
    zs, zo, zr = s["zs"], s["zo"], s["zr"]

    def conv(taps, weight, columns, out):
        width = columns.size

        def step(m, _):
            rows = pl.ds(m * CHUNK, CHUNK)
            total = product(taps[0, rows], weight[0, :, columns])
            total = total + product(taps[1, rows], weight[1, :, columns])
            out[rows, :width] = total + product(taps[2, rows], weight[2, :, columns])
            return 0

        lax.fori_loop(0, CHUNKS, step, 0)

    def pair_columns(which):
        return pl.ds(pl.multiple_of(which * 384, 128), 384)

    conv(u1, wp1, pair_columns(1 - core), zs)
    z1_copy = send(zs, zr, sems("z1"), 0, me.other_core)
    conv(u1, wp1, pair_columns(core), zo)
    z1_copy.wait_recv()

    def first_out(m, _):
        rows = pl.ds(m * CHUNK, CHUNK)
        value = x0p[rows].astype(F32) + (zo[rows] + zr[rows])
        rounded = value.astype(BF16)
        x1p[rows] = rounded
        u2[1, rows] = gelu_value(rounded.astype(F32)).astype(BF16)
        return 0

    u2_copies = []
    for m in range(CHUNKS):
        first_out(m, 0)
        rows = pl.ds(m * CHUNK, CHUNK)
        low = send.when(far_low, u2.at[1, rows], u2.at[2, rows], sems("u2h"), (0, m), me.along(-4))
        high = send.when(far_high, u2.at[1, rows], u2.at[0, rows], sems("u2h"), (1, m), me.along(4))
        u2_copies.append((far_high, low))
        u2_copies.append((far_low, high))
    c_chunk(2)
    c_chunk(3)
    arrived(firsts[2])
    arrived(firsts[3])
    assemble(1, wp2)

    def spread(full, name):
        return [send(full.at[t, core], full.at[t, core], sems(name), t, me.other_core) for t in (0, 2)]

    halo_arrived(g2_copies)
    g2_spread = spread(g2, "g2s")
    arrived(g2_core)

    d1, r1, d2, r2, d3, r3 = (s[n] for n in ("d1", "r1", "d2", "r2", "d3", "r3"))

    def weight_grad(b, taps, full):
        def step(tap, _):
            main = taps[tap, :, pl.ds(pl.multiple_of(half * 128, 128), 128)]
            tails = taps[tap, :, 256:384].astype(F32)
            tail = jnp.where(half == 0, tails[:, :64], tails[:, 64:]).astype(BF16)
            for c in (0, 1):
                upper = over_rows(main, full[1, c]).astype(BF16)
                lower = over_rows(tail, full[1, c]).astype(BF16)
                for t in range(3):
                    for i in range(8):
                        d1[b, tap * 72 + i * 6 + c * 3 + t] = upper[i * 16 : i * 16 + 16, t * 128 : t * 128 + 128]
                    for i in range(4):
                        d1[b, tap * 72 + (8 + i) * 6 + c * 3 + t] = lower[
                            i * 16 : i * 16 + 16, t * 128 : t * 128 + 128
                        ]
            return 0

        lax.fori_loop(0, 3, step, 0)

    def reduce_first(b, p):
        i = 2 * b + p
        axis = AXES[p][0]
        here = me.coordinate(axis)
        return [
            send(
                d1.at[b, pl.ds(p * 108 + lax.rem(here + d, 4) * UNITS, UNITS)],
                r1.at[i, d - 1],
                sems("s1"),
                (i, d - 1),
                me.shifted(axis, d),
            )
            for d in (1, 2, 3)
        ]

    def reduce_second(b, p, copies):
        i = 2 * b + p
        arrived(copies)
        base = p * 108 + me.coordinate(AXES[p][0]) * UNITS

        def step(r, _):
            total = d1[b, pl.ds(base + r * 9, 9)].astype(F32)
            for d in range(3):
                total = total + r1[i, d, pl.ds(r * 9, 9)].astype(F32)
            d2[i, pl.ds(r * 9, 9)] = total.astype(BF16)
            return 0

        lax.fori_loop(0, 3, step, 0)
        d2[i, UNITS:] = jnp.zeros((32 - UNITS, 16, 128), BF16)
        axis = AXES[p][1]
        there = me.coordinate(axis)
        return [
            send(
                d2.at[i, pl.ds(lax.rem(there + d, 4) * 8, 8)], r2.at[i, d - 1], sems("s2"), (i, d - 1),
                me.shifted(axis, d),
            )
            for d in (1, 2, 3)
        ]

    def reduce_third(b, p, copies):
        i = 2 * b + p
        arrived(copies)
        there = me.coordinate(AXES[p][1])
        total = d2[i, pl.ds(there * 8, 8)].astype(F32)
        for d in range(3):
            total = total + r2[i, d].astype(F32)
        d3[i] = total.astype(BF16)
        return [
            send(d3.at[i, lax.rem(me.z + d, 8)], r3.at[i, d - 1], sems("s3"), (i, d - 1), me.shifted("z", d))
            for d in range(1, 8)
        ]

    gh, ge, gf = s["gh"], s["ge"], s["gf"]

    def reduced(b, p, copies):
        i = 2 * b + p
        arrived(copies)
        total = d3[i, me.z].astype(F32)
        for d in range(7):
            total = total + r3[i, d].astype(F32)
        gh[i, me.z] = (total * (1.0 / math.sqrt(BINS))).astype(BF16)
        return gather_lines(i, gh, "gz")

    arrived(g2_spread)
    v = s["v"]

    def back_two(m, _):
        rows = pl.ds(m * CHUNK, CHUNK)
        total = jnp.zeros((CHUNK, 384), F32)
        for tap in range(3):
            for c in (0, 1):
                total = total + against(g2[tap, c, rows], wp2[tap, :, c * 384 : (c + 1) * 384])
        previous = x1p[rows].astype(F32)
        g1[1, core, rows] = (g2[1, core, rows].astype(F32) + gelu_slope(previous) * total).astype(BF16)
        return 0

    g1_core, g1_copies = [], []
    for m in range(CHUNKS):
        back_two(m, 0)
        rows = pl.ds(m * CHUNK, CHUNK)
        g1_core.append(send(g1.at[1, core, rows], g1.at[1, core, rows], sems("g1c"), m, me.other_core))
    arrived(g1_core)
    weight_grad(0, u1, g1)
    reduce = {}
    for p in (0, 1):
        reduce[0, p] = reduce_first(0, p)
    halo_arrived(u2_copies)
    weight_grad(1, u2, g2)
    for p in (0, 1):
        reduce[1, p] = reduce_first(1, p)
    for m in range(CHUNKS):
        rows = pl.ds(m * CHUNK, CHUNK)
        mine = g1.at[1, core, rows]
        low = send.when(near_low, mine, g1.at[0, core, rows], sems("g1h"), (0, m), me.along(-1))
        high = send.when(near_high, mine, g1.at[2, core, rows], sems("g1h"), (1, m), me.along(1))
        g1_copies.append((near_high, low))
        g1_copies.append((near_low, high))

    def own_columns(which):
        return pl.ds(pl.multiple_of(which * 384 + half * 128, 128), 128), pl.ds(
            pl.multiple_of(which * 384 + 256, 128), 128
        )

    ys, yo, yr = s["ys"], s["yo"], s["yr"]

    def conv_own(which, out):
        main, tails = own_columns(which)

        def step(m, _):
            rows = pl.ds(m * CHUNK, CHUNK)
            for at, columns in ((0, main), (128, tails)):
                total = product(u2[0, rows], wp2[0, :, columns])
                total = total + product(u2[1, rows], wp2[1, :, columns])
                out[rows, at : at + 128] = total + product(u2[2, rows], wp2[2, :, columns])
            return 0

        lax.fori_loop(0, CHUNKS, step, 0)

    conv_own(1 - core, ys)
    z2_copy = send(ys, yr, sems("z2"), 0, me.other_core)
    conv_own(core, yo)
    z2_copy.wait_recv()

    main_tile = pl.ds(pl.multiple_of(half * 128, 128), 128)

    def own_tail(tile):
        return jnp.where(half == 0, tile[:, :64], tile[:, 64:])

    def put(out, rows, main, tail):
        main, tail = main.astype(BF16), tail.astype(BF16)

        @pl.when(core == 0)
        def _():
            out[rows, 0:128] = main
            out[rows, 128:192] = tail

        @pl.when(core == 1)
        def _():
            out[rows] = jnp.concatenate([tail, main], axis=1)

    def second_out(m, _):
        rows = pl.ds(m * CHUNK, CHUNK)
        main = x1p[rows, main_tile].astype(F32) + (yo[rows, 0:128] + yr[rows, 0:128])
        tails = x1p[rows, 256:384].astype(F32) + (yo[rows, 128:256] + yr[rows, 128:256])
        put(act_out, rows, main, own_tail(tails))
        return 0

    lax.fori_loop(0, CHUNKS, second_out, 0)

    for b, p in parts:
        reduce[b, p] = reduce_second(b, p, reduce[b, p])
    for b, p in parts:
        reduce[b, p] = reduce_third(b, p, reduce[b, p])
    halo_arrived(g1_copies)
    g1_spread = spread(g1, "g1s")
    for b, p in parts:
        reduce[b, p] = reduced(b, p, reduce[b, p])

    arrived(g1_spread)

    def back_one(m, _):
        rows = pl.ds(m * CHUNK, CHUNK)
        main = jnp.zeros((CHUNK, 128), F32)
        tails = jnp.zeros((CHUNK, 128), F32)
        for tap in range(3):
            for c in (0, 1):
                grad = g1[tap, c, rows]
                main = main + against(grad, wp1[tap, main_tile, c * 384 : (c + 1) * 384])
                tails = tails + against(grad, wp1[tap, 256:384, c * 384 : (c + 1) * 384])
        main = g1[1, core, rows, main_tile].astype(F32) + gelu_slope(x0p[rows, main_tile].astype(F32)) * main
        tails = g1[1, core, rows, 256:384].astype(F32) + gelu_slope(x0p[rows, 256:384].astype(F32)) * tails
        put(grad_out, rows, main, own_tail(tails))
        return 0

    lax.fori_loop(0, CHUNKS, back_one, 0)

    for b, p in parts:
        arrived(reduce[b, p])
        reduce[b, p] = gather_second(2 * b + p, p, gh, ge, "e2")
    for b, p in parts:
        arrived(reduce[b, p])
        reduce[b, p] = gather_first(b, p, ge, gf, "e1")

    def unpack(b, out):
        def step(k, _):
            tap, natural = lax.div(k, 12), lax.rem(k, 12)
            row = lax.rem(natural + 12 - 4 * core, 12)
            tiles = [gf[b, tap * 72 + row * 6 + t] for t in range(6)]
            low, high = tiles[2], tiles[5]
            ordered = (
                tiles[0],
                jnp.concatenate([low[:, :64], high[:, :64]], axis=1),
                tiles[3],
                tiles[1],
                jnp.concatenate([low[:, 64:], high[:, 64:]], axis=1),
                tiles[4],
            )
            rows = pl.ds(pl.multiple_of(natural * 16, 16), 16)
            for t in range(6):
                out[tap, rows, t * 128 : (t + 1) * 128] = ordered[t]
            return 0

        lax.fori_loop(0, 36, step, 0)

    for b, out in ((0, near_out), (1, far_out)):
        arrived(reduce[b, 0])
        arrived(reduce[b, 1])
        unpack(b, out)
    send.finish()


def buffers():
    table = {}

    def keep(name, *shape, dtype=BF16):
        table[name] = pltpu.VMEM(shape, dtype)

    def pair(name, *shape):
        table[name + "_s"] = pltpu.SemaphoreType.DMA(shape)
        table[name + "_r"] = pltpu.SemaphoreType.DMA(shape)

    for name in ("xs", "xr", "cs", "cr"):
        keep(name, CHUNKS, CHUNK + 64, 128)
    keep("x0p", ROWS, 384)
    keep("x1p", ROWS, 384)
    keep("u1", 3, ROWS, 384)
    keep("u2", 3, ROWS, 384)
    keep("g2", 3, 2, ROWS, 384)
    keep("g1", 3, 2, ROWS, 384)
    keep("wp1", 3, 384, 768)
    keep("wp2", 3, 384, 768)
    for name in ("zs", "zo", "zr", "v"):
        keep(name, ROWS, 384, dtype=F32)
    for name in ("ys", "yo", "yr"):
        keep(name, ROWS, 256, dtype=F32)
    keep("wu", 4, 16, 128)
    keep("wh", 4, 8, 16, 128)
    keep("we", 4, 32, 16, 128)
    keep("wf", 2, 216, 16, 128)
    keep("d1", 2, 216, 16, 128)
    keep("r1", 4, 3, UNITS, 16, 128)
    keep("d2", 4, 32, 16, 128)
    keep("r2", 4, 3, 8, 16, 128)
    keep("d3", 4, 8, 16, 128)
    keep("r3", 4, 7, 16, 128)
    keep("gh", 4, 8, 16, 128)
    keep("ge", 4, 32, 16, 128)
    keep("gf", 2, 216, 16, 128)
    pair("wx", 4)
    pair("xx", CHUNKS)
    pair("cx", CHUNKS)
    for name in ("wz", "gz", "s3"):
        pair(name, 4, 7)
    for name in ("w2", "w1", "s1", "s2", "e2", "e1"):
        pair(name, 4, 3)
    for name in ("u1h", "u2h", "g1h", "g2h"):
        pair(name, 2, CHUNKS)
    for name in ("g2c", "g1c"):
        pair(name, CHUNKS)
    for name in ("g2s", "g1s"):
        pair(name, 3)
    pair("z1", 1)
    pair("z2", 1)
    return table


SCRATCH = buffers()


def body(inputs, cotangent, first_kernel_weight, second_kernel_weight):
    shapes = [jax.ShapeDtypeStruct((ROWS, 192), BF16)] * 2 + [jax.ShapeDtypeStruct((3, 192, 768), BF16)] * 2
    vmem = pl.BlockSpec(memory_space=pltpu.VMEM)
    return pl.pallas_call(
        kernel,
        out_shape=tuple(shapes),
        in_specs=[vmem] * 4,
        out_specs=(vmem,) * 4,
        scratch_shapes=list(SCRATCH.values()),
        compiler_params=pltpu.CompilerParams(
            collective_id=0, has_side_effects=True, vmem_limit_bytes=56 * 2**20
        ),
    )(inputs, cotangent, first_kernel_weight, second_kernel_weight)


def solution(mesh):
    return jax.shard_map(
        body,
        mesh=mesh,
        in_specs=(P("bins", "ch"), P("bins", "ch"), P(None, "ch", None), P(None, "ch", None)),
        out_specs=(P("bins", "ch"), P("bins", "ch"), P(None, "ch", None), P(None, "ch", None)),
        check_vma=False,
    )
```

```python
import math

import jax
import jax.numpy as jnp
from jax import lax
from jax.experimental import pallas as pl
from jax.experimental.pallas import tpu as pltpu
from jax.sharding import PartitionSpec as P

MESH = pl.DeviceIdType.MESH
ROWS = 512
CHUNKS = 4
CHUNK = ROWS // CHUNKS
UNITS = 27
WINDOW = 3
LAST_BIN = 127
BINS = 65536
F32, BF16 = jnp.float32, jnp.bfloat16

gelu_coeff = 0.7978845608

AXES = (("x", "y"), ("y", "x"))


def gelu_value(values):
    inner = gelu_coeff * (values + 0.044715 * values * values * values)
    return 0.5 * values * (1.0 + jnp.tanh(inner))


def gelu_slope(values):
    inner = gelu_coeff * (values + 0.044715 * values * values * values)
    tangent = jnp.tanh(inner)
    return 0.5 * (1.0 + tangent) + 0.5 * values * (1.0 - tangent * tangent) * gelu_coeff * (
        1.0 + 3.0 * 0.044715 * values * values
    )


def product(left, right):
    return jnp.dot(left, right, preferred_element_type=F32)


def against(left, right):
    return lax.dot_general(left, right, (((1,), (1,)), ((), ())), preferred_element_type=F32)


def over_rows(left, right):
    return lax.dot_general(left, right, (((0,), (0,)), ((), ())), preferred_element_type=F32)


class Place:
    def __init__(self):
        b = lax.axis_index("bins")
        self.b = b
        self.ch = lax.axis_index("ch")
        self.half = lax.div(self.ch, 2)
        self.core = lax.rem(self.ch, 2)
        self.x = lax.rem(b, 4)
        self.y = lax.rem(lax.div(b, 4), 4)
        self.z = lax.div(b, 16)
        self.other_half = (b, lax.rem(self.ch + 2, 4))
        self.other_core = (b, self.half * 2 + 1 - self.core)

    def shifted(self, axis, d):
        x, y, z = self.x, self.y, self.z
        if axis == "x":
            x = lax.rem(x + d, 4)
        elif axis == "y":
            y = lax.rem(y + d, 4)
        else:
            z = lax.rem(z + d, 8)
        return (z * 16 + y * 4 + x, self.ch)

    def along(self, distance):
        return (lax.rem(self.b + distance + 128, 128), self.ch)

    def coordinate(self, axis):
        return {"x": self.x, "y": self.y, "z": self.z}[axis]


def remote(src, dst, send_sem, recv_sem, target):
    return pltpu.make_async_remote_copy(
        src_ref=src,
        dst_ref=dst,
        send_sem=send_sem,
        recv_sem=recv_sem,
        device_id=target,
        device_id_type=MESH,
    )


class Sender:
    def __init__(self):
        self.pending = []

    def __call__(self, src, dst, sems, index, target):
        copy = remote(src, dst, sems[0].at[index], sems[1].at[index], target)
        copy.start()
        self.pending.append((None, copy))
        return copy

    def when(self, condition, src, dst, sems, index, target):
        copy = remote(src, dst, sems[0].at[index], sems[1].at[index], target)

        @pl.when(condition)
        def _():
            copy.start()

        self.pending.append((condition, copy))
        return copy

    def finish(self):
        for condition, copy in self.pending:
            if condition is None:
                copy.wait_send()
            else:
                pl.when(condition)(copy.wait_send)


def kernel(x_ref, c_ref, w1_ref, w2_ref, act_out, grad_out, near_out, far_out, *scratch):
    s = dict(zip(SCRATCH, scratch))
    me = Place()
    half, core = me.half, me.core
    send = Sender()
    barrier = pltpu.get_barrier_semaphore()

    def sems(name):
        return s[name + "_s"], s[name + "_r"], name

    near_low, near_high = me.b >= 1, me.b <= LAST_BIN - 1
    far_low, far_high = me.b >= 4, me.b <= LAST_BIN - 4

    for axis, n in (("x", 4), ("y", 4), ("z", 8)):
        for d in range(1, n):
            pl.semaphore_signal(barrier, inc=1, device_id=me.shifted(axis, d), device_id_type=MESH)
    pl.semaphore_signal(barrier, inc=1, device_id=me.other_half, device_id_type=MESH)
    pl.semaphore_signal(barrier, inc=1, device_id=me.other_core, device_id_type=MESH)
    for hops, condition in ((-1, near_low), (1, near_high), (-4, far_low), (4, far_high)):

        @pl.when(condition)
        def _(hops=hops):
            pl.semaphore_signal(barrier, inc=1, device_id=me.along(hops), device_id_type=MESH)

    xr, u1, x1, u2, g2, g1 = (s[n] for n in ("xr", "u1", "x1", "u2", "g2", "g1"))
    OWN, OTHER = 0, 1

    def own(array, tap):
        return array.at[tap, half, core]

    def other(array, tap):
        return array.at[tap, 1 - half, core]

    def blank(condition, ref):
        @pl.when(jnp.logical_not(condition))
        def _():
            ref[...] = jnp.zeros(ref.shape, ref.dtype)

    blank(near_low, u1.at[0])
    blank(near_high, u1.at[2])
    blank(far_low, u2.at[0])
    blank(far_high, u2.at[2])
    for array, low, high in ((g2, far_low, far_high), (g1, near_low, near_high)):
        for h in (0, 1):
            blank(high, array.at[0, h, core])
            blank(low, array.at[2, h, core])

    def lanes(m):
        return pl.ds(m * CHUNK, CHUNK)

    def own_gelu(r, _):
        rows = pl.ds(pl.multiple_of(r * 16, 16), 16)
        u1[1, OWN, rows] = gelu_value(x_ref[rows].astype(F32)).astype(BF16)
        return 0

    lax.fori_loop(0, 12, own_gelu, 0)

    wires = 15 + sum(c.astype(jnp.int32) for c in (near_low, near_high, far_low, far_high))
    pl.semaphore_wait(barrier, wires)

    weights = (w1_ref, w2_ref)
    parts = [(b, p) for b in (0, 1) for p in (0, 1)]

    wh, we, wf = s["wh"], s["we"], s["wf"]
    crossing = {}
    for b, p in parts:
        i = 2 * b + p
        first, second = me.coordinate(AXES[p][0]), me.coordinate(AXES[p][1])
        place = lax.rem(second * 8 + me.z, UNITS)
        unit = p * 108 + first * UNITS + place
        tap = lax.div(unit, 72)
        rest = lax.rem(unit, 72)
        row = pl.multiple_of(lax.div(rest, 6) * 16, 16)
        col = pl.multiple_of(lax.rem(rest, 6) * 128, 128)
        crossing[i] = send(
            weights[b].at[tap, pl.ds(row, 16), pl.ds(col, 128)], s["wu"].at[i], sems("wx"), i, me.other_half
        )

    crossed = []

    def cross():
        n = len(crossed)
        if n >= 2 * CHUNKS:
            return
        m = n % CHUNKS
        if n < CHUNKS:
            crossed.append(send(x_ref.at[:, lanes(m)], xr.at[:, lanes(m)], sems("xx"), m, me.other_half))
        else:
            crossed.append(
                send(c_ref.at[:, lanes(m)], own(g2, 1).at[:, lanes(m)], sems("cx"), m, me.other_half)
            )

    for _ in range(WINDOW):
        cross()

    def halo(low, high, distance, src, low_dst, high_dst, name, index):
        down = send.when(low, src, low_dst, sems(name), (0,) + index, me.along(-distance))
        up = send.when(high, src, high_dst, sems(name), (1,) + index, me.along(distance))
        return [(high, down), (low, up)]

    def halo_arrived(copies):
        for condition, copy in copies:
            pl.when(condition)(copy.wait_recv)

    def arrived(copies):
        for copy in copies:
            copy.wait_recv()

    u1_own = halo(near_low, near_high, 1, u1.at[1, OWN], u1.at[2, OWN], u1.at[0, OWN], "u1h", (CHUNKS,))
    g2_core = [send(c_ref, own(g2, 1), sems("g2c"), CHUNKS, me.other_core)]
    g2_own = halo(far_low, far_high, 4, c_ref, own(g2, 0), own(g2, 2), "g2h", (CHUNKS,))

    def own_cotangent(r, _):
        rows = pl.ds(pl.multiple_of(r * 16, 16), 16)
        g2[1, half, core, rows] = c_ref[rows]
        return 0

    lax.fori_loop(0, 12, own_cotangent, 0)

    def gather_lines(i, grouped, name):
        return [
            send(grouped.at[i, me.z], grouped.at[i, me.z], sems(name), (i, d - 1), me.shifted("z", d))
            for d in range(1, 8)
        ]

    def gather_second(i, p, grouped, wide, name):
        axis = AXES[p][1]
        there = pl.ds(me.coordinate(axis) * 8, 8)
        copies = [
            send(grouped.at[i], wide.at[i, there], sems(name), (i, d - 1), me.shifted(axis, d)) for d in (1, 2, 3)
        ]
        wide[i, there] = grouped[i]
        return copies

    def gather_first(b, p, wide, whole, name):
        axis = AXES[p][0]
        i = 2 * b + p
        here = pl.ds(p * 108 + me.coordinate(axis) * UNITS, UNITS)
        copies = [
            send(wide.at[i, pl.ds(0, UNITS)], whole.at[b, here], sems(name), (i, d - 1), me.shifted(axis, d))
            for d in (1, 2, 3)
        ]
        whole[b, here] = wide[i, :UNITS]
        return copies

    u1_copies = []

    def x_chunk(m):
        crossed[m].wait_recv()
        cross()
        u1[1, OTHER, :, lanes(m)] = gelu_value(xr[:, lanes(m)].astype(F32)).astype(BF16)
        src = u1.at[1, OTHER, :, lanes(m)]
        u1_copies.extend(
            halo(near_low, near_high, 1, src, u1.at[2, OTHER, :, lanes(m)], u1.at[0, OTHER, :, lanes(m)], "u1h", (m,))
        )

    g2_copies = {}

    def c_chunk(m):
        crossed[CHUNKS + m].wait_recv()
        cross()
        src = other(g2, 1).at[:, lanes(m)]
        g2_copies[m] = halo(
            far_low, far_high, 4, src, other(g2, 0).at[:, lanes(m)], other(g2, 2).at[:, lanes(m)], "g2h", (m,)
        )
        g2_core.append(send(src, src, sems("g2c"), m, me.other_core))

    g2_spread = []

    def g2_forward_own():
        halo_arrived(g2_own)
        for k, tap in enumerate((0, 2)):
            g2_spread.append(send(own(g2, tap), own(g2, tap), sems("g2s"), (k, CHUNKS), me.other_core))

    def g2_forward(m):
        halo_arrived(g2_copies[m])
        for k, tap in enumerate((0, 2)):
            src = other(g2, tap).at[:, lanes(m)]
            g2_spread.append(send(src, src, sems("g2s"), (k, m), me.other_core))

    zp, zr = s["zp"], s["zr"]

    def conv_one(weight, slot, add):
        def step(n, _):
            columns = pl.ds(pl.multiple_of(n * 128, 128), 128)
            rows = pl.ds(pl.multiple_of(n * 128, 128), 128)
            total = over_rows(weight[0, :, columns], u1[0, slot])
            total = total + over_rows(weight[1, :, columns], u1[1, slot])
            total = total + over_rows(weight[2, :, columns], u1[2, slot])
            if add:
                total = total + zp[rows]
            zp[rows] = total
            return 0

        lax.fori_loop(0, 6, step, 0)

    def assemble(b, out):
        def step(k, _):
            tap, i = lax.div(k, 12), lax.rem(k, 12)
            rows = pl.ds(pl.multiple_of(i * 16, 16), 16)
            for t in range(6):
                out[tap, rows, t * 128 : (t + 1) * 128] = wf[b, k * 6 + t]
            return 0

        lax.fori_loop(0, 36, step, 0)

    wo1, wo2 = s["wo1"], s["wo2"]
    lines, seconds, firsts = {}, {}, {}
    for b, p in parts:
        i = 2 * b + p
        crossing[i].wait_recv()
        wh[i, me.z] = s["wu"][i]
        lines[i] = gather_lines(i, wh, "wz")
    x_chunk(0)
    for b, p in parts:
        i = 2 * b + p
        arrived(lines[i])
        seconds[i] = gather_second(i, p, wh, we, "w2")
    x_chunk(1)
    for b, p in parts:
        i = 2 * b + p
        arrived(seconds[i])
        firsts[i] = gather_first(b, p, we, wf, "w1")
    x_chunk(2)
    halo_arrived(u1_own)
    conv_one(w1_ref, OWN, False)
    g2_forward_own()
    x_chunk(3)
    arrived(firsts[0])
    arrived(firsts[1])
    assemble(0, wo1)
    c_chunk(0)
    halo_arrived(u1_copies)
    conv_one(wo1, OTHER, True)

    def group_rows(h, c):
        return pl.ds(pl.multiple_of((h * 2 + c) * 192, 64), 192)

    z1 = [send(zp.at[group_rows(h, 1 - core)], zr.at[h], sems("z1"), h, me.other_core) for h in (0, 1)]
    c_chunk(1)
    arrived(z1)
    u2_copies = []

    def x1_chunk(m):
        for slot, h in ((OWN, half), (OTHER, 1 - half)):
            before = x_ref[:, lanes(m)] if slot == OWN else xr[:, lanes(m)]
            total = zp[group_rows(h, core), lanes(m)] + zr[h, :, lanes(m)]
            value = (before.astype(F32) + total).astype(BF16)
            x1[slot, :, lanes(m)] = value
            u2[1, slot, :, lanes(m)] = gelu_value(value.astype(F32)).astype(BF16)
        src = u2.at[1, :, :, lanes(m)]
        u2_copies.extend(
            halo(far_low, far_high, 4, src, u2.at[2, :, :, lanes(m)], u2.at[0, :, :, lanes(m)], "u2h", (m,))
        )

    for m in range(CHUNKS):
        x1_chunk(m)
    arrived(firsts[2])
    arrived(firsts[3])
    assemble(1, wo2)
    g2_forward(0)
    c_chunk(2)
    g2_forward(1)

    v = s["v"]

    def half_columns(h):
        return pl.ds(pl.multiple_of(h * 384, 128), 384)

    arrived(g2_core[:1])
    arrived(g2_spread[:2])
    for slot, weight in ((OWN, w2_ref), (OTHER, wo2)):
        total = product(weight[0, :, half_columns(half)], g2[0, half].reshape(384, ROWS))
        total = total + product(weight[1, :, half_columns(half)], g2[1, half].reshape(384, ROWS))
        v[slot] = total + product(weight[2, :, half_columns(half)], g2[2, half].reshape(384, ROWS))
    c_chunk(3)
    g2_forward(2)
    g2_forward(3)

    d1, r1, d2, r2, d3, r3 = (s[n] for n in ("d1", "r1", "d2", "r2", "d3", "r3"))

    def weight_grad(b, left, right):
        def step(tap, _):
            for h in (0, 1):
                value = against(left(tap), right(tap, h).reshape(384, ROWS)).astype(BF16)
                for t in range(3):
                    for i in range(12):
                        d1[b, tap * 72 + i * 6 + h * 3 + t] = value[i * 16 : i * 16 + 16, t * 128 : t * 128 + 128]
            return 0

        lax.fori_loop(0, 3, step, 0)

    def reduce_first(b, p):
        i = 2 * b + p
        axis = AXES[p][0]
        here = me.coordinate(axis)
        return [
            send(
                d1.at[b, pl.ds(p * 108 + lax.rem(here + d, 4) * UNITS, UNITS)],
                r1.at[i, d - 1],
                sems("s1"),
                (i, d - 1),
                me.shifted(axis, d),
            )
            for d in (1, 2, 3)
        ]

    def reduce_second(b, p, copies):
        i = 2 * b + p
        arrived(copies)
        base = p * 108 + me.coordinate(AXES[p][0]) * UNITS

        def step(r, _):
            total = d1[b, pl.ds(base + r * 9, 9)].astype(F32)
            for d in range(3):
                total = total + r1[i, d, pl.ds(r * 9, 9)].astype(F32)
            d2[i, pl.ds(r * 9, 9)] = total.astype(BF16)
            return 0

        lax.fori_loop(0, 3, step, 0)
        d2[i, UNITS:] = jnp.zeros((32 - UNITS, 16, 128), BF16)
        axis = AXES[p][1]
        there = me.coordinate(axis)
        return [
            send(
                d2.at[i, pl.ds(lax.rem(there + d, 4) * 8, 8)], r2.at[i, d - 1], sems("s2"), (i, d - 1),
                me.shifted(axis, d),
            )
            for d in (1, 2, 3)
        ]

    def reduce_third(b, p, copies):
        i = 2 * b + p
        arrived(copies)
        there = me.coordinate(AXES[p][1])
        total = d2[i, pl.ds(there * 8, 8)].astype(F32)
        for d in range(3):
            total = total + r2[i, d].astype(F32)
        d3[i] = total.astype(BF16)
        return [
            send(d3.at[i, lax.rem(me.z + d, 8)], r3.at[i, d - 1], sems("s3"), (i, d - 1), me.shifted("z", d))
            for d in range(1, 8)
        ]

    gh, ge, gf = s["gh"], s["ge"], s["gf"]

    def reduced(b, p, copies):
        i = 2 * b + p
        arrived(copies)
        total = d3[i, me.z].astype(F32)
        for d in range(7):
            total = total + r3[i, d].astype(F32)
        gh[i, me.z] = (total * (1.0 / math.sqrt(BINS))).astype(BF16)
        return gather_lines(i, gh, "gz")

    reduce = {}
    arrived(g2_core[1:])
    arrived(g2_spread[2:])
    g1_core = []

    def back_two(n):
        wide = pl.ds(n * 256, 256)
        for slot, weight, h in ((OWN, w2_ref, half), (OTHER, wo2, 1 - half)):
            total = v[slot, :, wide]
            for tap in range(3):
                grad = g2[tap, 1 - half, :, :, wide].reshape(384, 256)
                total = total + product(weight[tap, :, half_columns(1 - half)], grad)
            slope = gelu_slope(x1[slot, :, wide].astype(F32))
            g1[1, h, core, :, wide] = (g2[1, h, core, :, wide].astype(F32) + slope * total).astype(BF16)
        src = g1.at[1, :, core, :, wide]
        g1_core.append(send(src, src, sems("g1c"), n, me.other_core))

    back_two(0)
    back_two(1)
    weight_grad(1, lambda tap: u2[1, OWN], lambda tap, h: g2[tap, h])
    for p in (0, 1):
        reduce[1, p] = reduce_first(1, p)
    arrived(g1_core)
    weight_grad(0, lambda tap: u1[tap, OWN], lambda tap, h: g1[1, h])
    for p in (0, 1):
        reduce[0, p] = reduce_first(0, p)
    src = g1.at[1, :, core]
    g1_copies = halo(near_low, near_high, 1, src, g1.at[0, :, core], g1.at[2, :, core], "g1h", (0,))

    yp, yr = s["yp"], s["yr"]

    def conv_two(n, _):
        columns = pl.ds(pl.multiple_of(half * 384 + n * 128, 128), 128)
        total = jnp.zeros((128, ROWS), F32)
        for tap in range(3):
            total = total + over_rows(w2_ref[tap, :, columns], u2[tap, OWN])
            total = total + over_rows(wo2[tap, :, columns], u2[tap, OTHER])
        yp[pl.ds(pl.multiple_of(n * 128, 128), 128)] = total
        return 0

    order = [(b, p) for b in (1, 0) for p in (0, 1)]
    halo_arrived(u2_copies)
    lax.fori_loop(0, 3, conv_two, 0)
    z2 = send(yp.at[pl.ds(pl.multiple_of((1 - core) * 192, 64), 192)], yr, sems("z2"), 0, me.other_core)
    for b, p in order:
        reduce[b, p] = reduce_second(b, p, reduce[b, p])
    z2.wait_recv()
    for m in range(CHUNKS):
        total = yp[pl.ds(pl.multiple_of(core * 192, 64), 192), lanes(m)] + yr[:, lanes(m)]
        act_out[:, lanes(m)] = (x1[OWN, :, lanes(m)].astype(F32) + total).astype(BF16)
    for b, p in order:
        reduce[b, p] = reduce_third(b, p, reduce[b, p])
    halo_arrived(g1_copies)
    g1_spread = [send(g1.at[t, :, core], g1.at[t, :, core], sems("g1s"), k, me.other_core) for k, t in ((0, 0), (1, 2))]
    for b, p in order:
        reduce[b, p] = reduced(b, p, reduce[b, p])

    arrived(g1_spread)

    for n in (0, 1):
        wide = pl.ds(n * 256, 256)
        total = product(w1_ref[0], g1[0, :, :, :, wide].reshape(768, 256))
        total = total + product(w1_ref[1], g1[1, :, :, :, wide].reshape(768, 256))
        total = total + product(w1_ref[2], g1[2, :, :, :, wide].reshape(768, 256))
        slope = gelu_slope(x_ref[:, wide].astype(F32))
        grad_out[:, wide] = (g1[1, half, core, :, wide].astype(F32) + slope * total).astype(BF16)

    for b, p in order:
        arrived(reduce[b, p])
        reduce[b, p] = gather_second(2 * b + p, p, gh, ge, "e2")
    for b, p in order:
        arrived(reduce[b, p])
        reduce[b, p] = gather_first(b, p, ge, gf, "e1")

    def unpack(b, out):
        def step(k, _):
            tap, i = lax.div(k, 12), lax.rem(k, 12)
            rows = pl.ds(pl.multiple_of(i * 16, 16), 16)
            for t in range(6):
                out[tap, rows, t * 128 : (t + 1) * 128] = gf[b, k * 6 + t]
            return 0

        lax.fori_loop(0, 36, step, 0)

    for b, out in ((1, far_out), (0, near_out)):
        arrived(reduce[b, 0])
        arrived(reduce[b, 1])
        unpack(b, out)
    send.finish()


def buffers():
    table = {}

    def keep(name, *shape, dtype=BF16):
        table[name] = pltpu.VMEM(shape, dtype)

    def pair(name, *shape):
        table[name + "_s"] = pltpu.SemaphoreType.DMA(shape)
        table[name + "_r"] = pltpu.SemaphoreType.DMA(shape)

    keep("xr", 192, ROWS)
    keep("x1", 2, 192, ROWS)
    keep("u1", 3, 2, 192, ROWS)
    keep("u2", 3, 2, 192, ROWS)
    keep("g2", 3, 2, 2, 192, ROWS)
    keep("g1", 3, 2, 2, 192, ROWS)
    keep("wo1", 3, 192, 768)
    keep("wo2", 3, 192, 768)
    keep("zp", 768, ROWS, dtype=F32)
    keep("zr", 2, 192, ROWS, dtype=F32)
    keep("v", 2, 192, ROWS, dtype=F32)
    keep("yp", 384, ROWS, dtype=F32)
    keep("yr", 192, ROWS, dtype=F32)
    keep("wu", 4, 16, 128)
    keep("wh", 4, 8, 16, 128)
    keep("we", 4, 32, 16, 128)
    keep("wf", 2, 216, 16, 128)
    keep("d1", 2, 216, 16, 128)
    keep("r1", 4, 3, UNITS, 16, 128)
    keep("d2", 4, 32, 16, 128)
    keep("r2", 4, 3, 8, 16, 128)
    keep("d3", 4, 8, 16, 128)
    keep("r3", 4, 7, 16, 128)
    keep("gh", 4, 8, 16, 128)
    keep("ge", 4, 32, 16, 128)
    keep("gf", 2, 216, 16, 128)
    pair("wx", 4)
    pair("xx", CHUNKS)
    pair("cx", CHUNKS)
    for name in ("wz", "gz", "s3"):
        pair(name, 4, 7)
    for name in ("w2", "w1", "s1", "s2", "e2", "e1"):
        pair(name, 4, 3)
    for name in ("u1h", "g2h", "g2s"):
        pair(name, 2, CHUNKS + 1)
    pair("u2h", 2, CHUNKS)
    pair("g1h", 2, 1)
    pair("g2c", CHUNKS + 1)
    for name in ("g1c", "g1s", "z1"):
        pair(name, 2)
    pair("z2", 1)
    return table


SCRATCH = buffers()


def body(inputs, cotangent, first_kernel_weight, second_kernel_weight):
    shapes = [jax.ShapeDtypeStruct((192, ROWS), BF16)] * 2 + [jax.ShapeDtypeStruct((3, 192, 768), BF16)] * 2
    vmem = pl.BlockSpec(memory_space=pltpu.VMEM)
    act, grad, near, far = pl.pallas_call(
        kernel,
        out_shape=tuple(shapes),
        in_specs=[vmem] * 4,
        out_specs=(vmem,) * 4,
        scratch_shapes=list(SCRATCH.values()),
        compiler_params=pltpu.CompilerParams(
            collective_id=0, has_side_effects=True, vmem_limit_bytes=56 * 2**20
        ),
    )(inputs.T, cotangent.T, first_kernel_weight, second_kernel_weight)
    return act.T, grad.T, near, far


def solution(mesh):
    return jax.shard_map(
        body,
        mesh=mesh,
        in_specs=(P("bins", "ch"), P("bins", "ch"), P(None, "ch", None), P(None, "ch", None)),
        out_specs=(P("bins", "ch"), P("bins", "ch"), P(None, "ch", None), P(None, "ch", None)),
        check_vma=False,
    )
```

```python
import math

import jax
import jax.numpy as jnp
from jax import lax
from jax.experimental import pallas as pl
from jax.experimental.pallas import tpu as pltpu
from jax.sharding import PartitionSpec as P

MESH = pl.DeviceIdType.MESH
ROWS = 512
CHUNKS = 4
CHUNK = ROWS // CHUNKS
UNITS = 27
WINDOW = 3
LAST_BIN = 127
BINS = 65536
F32, BF16 = jnp.float32, jnp.bfloat16

gelu_coeff = 0.7978845608

AXES = (("x", "y"), ("y", "x"))


def gelu_value(values):
    inner = gelu_coeff * (values + 0.044715 * values * values * values)
    return 0.5 * values * (1.0 + jnp.tanh(inner))


def gelu_slope(values):
    inner = gelu_coeff * (values + 0.044715 * values * values * values)
    tangent = jnp.tanh(inner)
    return 0.5 * (1.0 + tangent) + 0.5 * values * (1.0 - tangent * tangent) * gelu_coeff * (
        1.0 + 3.0 * 0.044715 * values * values
    )


def product(left, right):
    return jnp.dot(left, right, preferred_element_type=F32)


def against(left, right):
    return lax.dot_general(left, right, (((1,), (1,)), ((), ())), preferred_element_type=F32)


def over_rows(left, right):
    return lax.dot_general(left, right, (((0,), (0,)), ((), ())), preferred_element_type=F32)


class Place:
    def __init__(self):
        b = lax.axis_index("bins")
        self.b = b
        self.ch = lax.axis_index("ch")
        self.half = lax.div(self.ch, 2)
        self.core = lax.rem(self.ch, 2)
        self.x = lax.rem(b, 4)
        self.y = lax.rem(lax.div(b, 4), 4)
        self.z = lax.div(b, 16)
        self.other_half = (b, lax.rem(self.ch + 2, 4))
        self.other_core = (b, self.half * 2 + 1 - self.core)

    def shifted(self, axis, d):
        x, y, z = self.x, self.y, self.z
        if axis == "x":
            x = lax.rem(x + d, 4)
        elif axis == "y":
            y = lax.rem(y + d, 4)
        else:
            z = lax.rem(z + d, 8)
        return (z * 16 + y * 4 + x, self.ch)

    def along(self, distance):
        return (lax.rem(self.b + distance + 128, 128), self.ch)

    def coordinate(self, axis):
        return {"x": self.x, "y": self.y, "z": self.z}[axis]


def remote(src, dst, send_sem, recv_sem, target):
    return pltpu.make_async_remote_copy(
        src_ref=src,
        dst_ref=dst,
        send_sem=send_sem,
        recv_sem=recv_sem,
        device_id=target,
        device_id_type=MESH,
    )


class Sender:
    def __init__(self):
        self.pending = []

    def __call__(self, src, dst, sems, index, target):
        copy = remote(src, dst, sems[0].at[index], sems[1].at[index], target)
        copy.start()
        self.pending.append((None, copy))
        return copy

    def when(self, condition, src, dst, sems, index, target):
        copy = remote(src, dst, sems[0].at[index], sems[1].at[index], target)

        @pl.when(condition)
        def _():
            copy.start()

        self.pending.append((condition, copy))
        return copy

    def finish(self):
        for condition, copy in self.pending:
            if condition is None:
                copy.wait_send()
            else:
                pl.when(condition)(copy.wait_send)


def kernel(x_ref, c_ref, w1_ref, w2_ref, act_out, grad_out, near_out, far_out, *scratch):
    s = dict(zip(SCRATCH, scratch))
    me = Place()
    half, core = me.half, me.core
    send = Sender()
    barrier = pltpu.get_barrier_semaphore()

    def sems(name):
        return s[name + "_s"], s[name + "_r"], name

    near_low, near_high = me.b >= 1, me.b <= LAST_BIN - 1
    far_low, far_high = me.b >= 4, me.b <= LAST_BIN - 4

    for axis, n in (("x", 4), ("y", 4), ("z", 8)):
        for d in range(1, n):
            pl.semaphore_signal(barrier, inc=1, device_id=me.shifted(axis, d), device_id_type=MESH)
    pl.semaphore_signal(barrier, inc=1, device_id=me.other_half, device_id_type=MESH)
    pl.semaphore_signal(barrier, inc=1, device_id=me.other_core, device_id_type=MESH)
    for hops, condition in ((-1, near_low), (1, near_high), (-4, far_low), (4, far_high)):

        @pl.when(condition)
        def _(hops=hops):
            pl.semaphore_signal(barrier, inc=1, device_id=me.along(hops), device_id_type=MESH)

    xr, u1, x1, u2, g2, g1 = (s[n] for n in ("xr", "u1", "x1", "u2", "g2", "g1"))
    OWN, OTHER = 0, 1

    def own(array, tap):
        return array.at[tap, half, core]

    def other(array, tap):
        return array.at[tap, 1 - half, core]

    def blank(condition, ref):
        @pl.when(jnp.logical_not(condition))
        def _():
            ref[...] = jnp.zeros(ref.shape, ref.dtype)

    blank(near_low, u1.at[0])
    blank(near_high, u1.at[2])
    qs, qr, ts, tr = s["qs"], s["qr"], s["ts"], s["tr"]
    blank(near_high, qr.at[0])
    blank(near_low, qr.at[1])
    blank(far_low, tr.at[0])
    blank(far_high, tr.at[1])
    for h in (0, 1):
        blank(far_high, g2.at[0, h, core])
        blank(far_low, g2.at[2, h, core])

    def lanes(m):
        return pl.ds(m * CHUNK, CHUNK)

    def own_gelu(r, _):
        rows = pl.ds(pl.multiple_of(r * 16, 16), 16)
        u1[1, OWN, rows] = gelu_value(x_ref[rows].astype(F32)).astype(BF16)
        return 0

    lax.fori_loop(0, 12, own_gelu, 0)

    wires = 15 + sum(c.astype(jnp.int32) for c in (near_low, near_high, far_low, far_high))
    pl.semaphore_wait(barrier, wires)

    weights = (w1_ref, w2_ref)
    parts = [(b, p) for b in (0, 1) for p in (0, 1)]

    wh, we, wf = s["wh"], s["we"], s["wf"]
    crossing = {}
    for b, p in parts:
        i = 2 * b + p
        first, second = me.coordinate(AXES[p][0]), me.coordinate(AXES[p][1])
        place = lax.rem(second * 8 + me.z, UNITS)
        unit = p * 108 + first * UNITS + place
        tap = lax.div(unit, 72)
        rest = lax.rem(unit, 72)
        row = pl.multiple_of(lax.div(rest, 6) * 16, 16)
        col = pl.multiple_of(lax.rem(rest, 6) * 128, 128)
        crossing[i] = send(
            weights[b].at[tap, pl.ds(row, 16), pl.ds(col, 128)], s["wu"].at[i], sems("wx"), i, me.other_half
        )

    crossed = []

    def cross():
        n = len(crossed)
        if n >= 2 * CHUNKS:
            return
        m = n % CHUNKS
        if n < CHUNKS:
            crossed.append(send(x_ref.at[:, lanes(m)], xr.at[:, lanes(m)], sems("xx"), m, me.other_half))
        else:
            crossed.append(
                send(c_ref.at[:, lanes(m)], own(g2, 1).at[:, lanes(m)], sems("cx"), m, me.other_half)
            )

    for _ in range(WINDOW):
        cross()

    def halo(low, high, distance, src, low_dst, high_dst, name, index):
        down = send.when(low, src, low_dst, sems(name), (0,) + index, me.along(-distance))
        up = send.when(high, src, high_dst, sems(name), (1,) + index, me.along(distance))
        return [(high, down), (low, up)]

    def halo_arrived(copies):
        for condition, copy in copies:
            pl.when(condition)(copy.wait_recv)

    def arrived(copies):
        for copy in copies:
            copy.wait_recv()

    u1_own = halo(near_low, near_high, 1, u1.at[1, OWN], u1.at[2, OWN], u1.at[0, OWN], "u1h", (CHUNKS,))
    g2_core = [send(c_ref, own(g2, 1), sems("g2c"), CHUNKS, me.other_core)]

    def own_cotangent(r, _):
        rows = pl.ds(pl.multiple_of(r * 16, 16), 16)
        g2[1, half, core, rows] = c_ref[rows]
        return 0

    lax.fori_loop(0, 12, own_cotangent, 0)

    def gather_lines(i, grouped, name):
        return [
            send(grouped.at[i, me.z], grouped.at[i, me.z], sems(name), (i, d - 1), me.shifted("z", d))
            for d in range(1, 8)
        ]

    def gather_second(i, p, grouped, wide, name):
        axis = AXES[p][1]
        there = pl.ds(me.coordinate(axis) * 8, 8)
        copies = [
            send(grouped.at[i], wide.at[i, there], sems(name), (i, d - 1), me.shifted(axis, d)) for d in (1, 2, 3)
        ]
        wide[i, there] = grouped[i]
        return copies

    def gather_first(b, p, wide, whole, name):
        axis = AXES[p][0]
        i = 2 * b + p
        here = pl.ds(p * 108 + me.coordinate(axis) * UNITS, UNITS)
        copies = [
            send(wide.at[i, pl.ds(0, UNITS)], whole.at[b, here], sems(name), (i, d - 1), me.shifted(axis, d))
            for d in (1, 2, 3)
        ]
        whole[b, here] = wide[i, :UNITS]
        return copies

    u1_copies = []

    def x_chunk(m):
        crossed[m].wait_recv()
        cross()
        u1[1, OTHER, :, lanes(m)] = gelu_value(xr[:, lanes(m)].astype(F32)).astype(BF16)
        src = u1.at[1, OTHER, :, lanes(m)]
        u1_copies.extend(
            halo(near_low, near_high, 1, src, u1.at[2, OTHER, :, lanes(m)], u1.at[0, OTHER, :, lanes(m)], "u1h", (m,))
        )

    g2_copies = {}

    def c_chunk(m):
        crossed[CHUNKS + m].wait_recv()
        cross()
        src = other(g2, 1).at[:, lanes(m)]
        g2_copies[m] = halo(
            far_low, far_high, 4, src, other(g2, 0).at[:, lanes(m)], other(g2, 2).at[:, lanes(m)], "g2h", (m,)
        )
        g2_core.append(send(src, src, sems("g2c"), m, me.other_core))

    g2_spread = []

    def g2_forward_own():
        halo_arrived(g2_own)
        for k, tap in enumerate((0, 2)):
            g2_spread.append(send(own(g2, tap), own(g2, tap), sems("g2s"), (k, CHUNKS), me.other_core))

    def g2_forward(m):
        halo_arrived(g2_copies[m])
        for k, tap in enumerate((0, 2)):
            src = other(g2, tap).at[:, lanes(m)]
            g2_spread.append(send(src, src, sems("g2s"), (k, m), me.other_core))

    zp, zr = s["zp"], s["zr"]

    def conv_one(weight, slot, add):
        def step(n, _):
            columns = pl.ds(pl.multiple_of(n * 128, 128), 128)
            rows = pl.ds(pl.multiple_of(n * 128, 128), 128)
            total = over_rows(weight[0, :, columns], u1[0, slot])
            total = total + over_rows(weight[1, :, columns], u1[1, slot])
            total = total + over_rows(weight[2, :, columns], u1[2, slot])
            if add:
                total = total + zp[rows]
            zp[rows] = total
            return 0

        lax.fori_loop(0, 6, step, 0)

    def assemble(b, out):
        def step(k, _):
            tap, i = lax.div(k, 12), lax.rem(k, 12)
            rows = pl.ds(pl.multiple_of(i * 16, 16), 16)
            for t in range(6):
                out[tap, rows, t * 128 : (t + 1) * 128] = wf[b, k * 6 + t]
            return 0

        lax.fori_loop(0, 36, step, 0)

    wo1, wo2 = s["wo1"], s["wo2"]
    lines, seconds, firsts = {}, {}, {}
    for b, p in parts:
        i = 2 * b + p
        crossing[i].wait_recv()
        wh[i, me.z] = s["wu"][i]
        lines[i] = gather_lines(i, wh, "wz")
    x_chunk(0)
    for b, p in parts:
        i = 2 * b + p
        arrived(lines[i])
        seconds[i] = gather_second(i, p, wh, we, "w2")
    x_chunk(1)
    for b, p in parts:
        i = 2 * b + p
        arrived(seconds[i])
        firsts[i] = gather_first(b, p, we, wf, "w1")
    x_chunk(2)
    halo_arrived(u1_own)
    conv_one(w1_ref, OWN, False)
    x_chunk(3)
    g2_own = halo(far_low, far_high, 4, c_ref, own(g2, 0), own(g2, 2), "g2h", (CHUNKS,))
    arrived(firsts[0])
    arrived(firsts[1])
    assemble(0, wo1)
    c_chunk(0)
    halo_arrived(u1_copies)
    conv_one(wo1, OTHER, True)

    def group_rows(h, c):
        return pl.ds(pl.multiple_of((h * 2 + c) * 192, 64), 192)

    z1 = [send(zp.at[group_rows(h, 1 - core)], zr.at[h], sems("z1"), h, me.other_core) for h in (0, 1)]
    c_chunk(1)
    arrived(z1)

    def x1_chunk(m):
        for slot, h in ((OWN, half), (OTHER, 1 - half)):
            before = x_ref[:, lanes(m)] if slot == OWN else xr[:, lanes(m)]
            total = zp[group_rows(h, core), lanes(m)] + zr[h, :, lanes(m)]
            value = (before.astype(F32) + total).astype(BF16)
            x1[slot, :, lanes(m)] = value
            u2[slot, :, lanes(m)] = gelu_value(value.astype(F32)).astype(BF16)

    for m in range(CHUNKS):
        x1_chunk(m)
    arrived(firsts[2])
    arrived(firsts[3])
    assemble(1, wo2)
    g2_forward_own()
    g2_forward(0)
    c_chunk(2)
    g2_forward(1)

    v = s["v"]

    def half_columns(h):
        return pl.ds(pl.multiple_of(h * 384, 128), 384)

    arrived(g2_core[:1])
    arrived(g2_spread[:2])
    for slot, weight in ((OWN, w2_ref), (OTHER, wo2)):
        total = product(weight[0, :, half_columns(half)], g2[0, half].reshape(384, ROWS))
        total = total + product(weight[1, :, half_columns(half)], g2[1, half].reshape(384, ROWS))
        v[slot] = total + product(weight[2, :, half_columns(half)], g2[2, half].reshape(384, ROWS))
    c_chunk(3)
    g2_forward(2)
    g2_forward(3)

    d1, r1, d2, r2, d3, r3 = (s[n] for n in ("d1", "r1", "d2", "r2", "d3", "r3"))

    def weight_grad(b, left, right):
        def step(tap, _):
            for h in (0, 1):
                value = against(left(tap), right(tap, h).reshape(384, ROWS)).astype(BF16)
                for t in range(3):
                    for i in range(12):
                        d1[b, tap * 72 + i * 6 + h * 3 + t] = value[i * 16 : i * 16 + 16, t * 128 : t * 128 + 128]
            return 0

        lax.fori_loop(0, 3, step, 0)

    def reduce_first(b, p):
        i = 2 * b + p
        axis = AXES[p][0]
        here = me.coordinate(axis)
        return [
            send(
                d1.at[b, pl.ds(p * 108 + lax.rem(here + d, 4) * UNITS, UNITS)],
                r1.at[i, d - 1],
                sems("s1"),
                (i, d - 1),
                me.shifted(axis, d),
            )
            for d in (1, 2, 3)
        ]

    def reduce_second(b, p, copies):
        i = 2 * b + p
        arrived(copies)
        base = p * 108 + me.coordinate(AXES[p][0]) * UNITS

        def step(r, _):
            total = d1[b, pl.ds(base + r * 9, 9)].astype(F32)
            for d in range(3):
                total = total + r1[i, d, pl.ds(r * 9, 9)].astype(F32)
            d2[i, pl.ds(r * 9, 9)] = total.astype(BF16)
            return 0

        lax.fori_loop(0, 3, step, 0)
        d2[i, UNITS:] = jnp.zeros((32 - UNITS, 16, 128), BF16)
        axis = AXES[p][1]
        there = me.coordinate(axis)
        return [
            send(
                d2.at[i, pl.ds(lax.rem(there + d, 4) * 8, 8)], r2.at[i, d - 1], sems("s2"), (i, d - 1),
                me.shifted(axis, d),
            )
            for d in (1, 2, 3)
        ]

    def reduce_third(b, p, copies):
        i = 2 * b + p
        arrived(copies)
        there = me.coordinate(AXES[p][1])
        total = d2[i, pl.ds(there * 8, 8)].astype(F32)
        for d in range(3):
            total = total + r2[i, d].astype(F32)
        d3[i] = total.astype(BF16)
        return [
            send(d3.at[i, lax.rem(me.z + d, 8)], r3.at[i, d - 1], sems("s3"), (i, d - 1), me.shifted("z", d))
            for d in range(1, 8)
        ]

    gh, ge, gf = s["gh"], s["ge"], s["gf"]

    def reduced(b, p, copies):
        i = 2 * b + p
        arrived(copies)
        total = d3[i, me.z].astype(F32)
        for d in range(7):
            total = total + r3[i, d].astype(F32)
        gh[i, me.z] = (total * (1.0 / math.sqrt(BINS))).astype(BF16)
        return gather_lines(i, gh, "gz")

    reduce = {}
    arrived(g2_core[1:])
    arrived(g2_spread[2:])
    g1_core = []

    def back_two(n):
        wide = pl.ds(n * 256, 256)
        for slot, weight, h in ((OWN, w2_ref, half), (OTHER, wo2, 1 - half)):
            total = v[slot, :, wide]
            for tap in range(3):
                grad = g2[tap, 1 - half, :, :, wide].reshape(384, 256)
                total = total + product(weight[tap, :, half_columns(1 - half)], grad)
            slope = gelu_slope(x1[slot, :, wide].astype(F32))
            g1[h, core, :, wide] = (g2[1, h, core, :, wide].astype(F32) + slope * total).astype(BF16)
        src = g1.at[:, core, :, wide]
        g1_core.append(send(src, src, sems("g1c"), n, me.other_core))

    weight_grad(1, lambda tap: u2[OWN], lambda tap, h: g2[tap, h])
    for p in (0, 1):
        reduce[1, p] = reduce_first(1, p)
    back_two(0)
    back_two(1)
    arrived(g1_core)
    weight_grad(0, lambda tap: u1[tap, OWN], lambda tap, h: g1[h])
    for p in (0, 1):
        reduce[0, p] = reduce_first(0, p)

    yp, yr = s["yp"], s["yr"]

    def conv_two(n, _):
        columns = pl.ds(pl.multiple_of(half * 384 + n * 128, 128), 128)
        for tap in range(3):
            total = over_rows(w2_ref[tap, :, columns], u2[OWN]) + over_rows(wo2[tap, :, columns], u2[OTHER])
            yp[tap, pl.ds(pl.multiple_of(n * 128, 128), 128)] = total
        return 0

    for k, tap in enumerate((0, 2)):
        qs[k] = product(w1_ref[tap], g1[...].reshape(768, ROWS)).astype(BF16)
    down = send.when(near_low, qs.at[0], qr.at[0], sems("g1h"), (0, 0), me.along(-1))
    up = send.when(near_high, qs.at[1], qr.at[1], sems("g1h"), (1, 0), me.along(1))
    g1_copies = [(near_high, down), (near_low, up)]
    lax.fori_loop(0, 3, conv_two, 0)
    z2 = send(yp.at[:, pl.ds(pl.multiple_of((1 - core) * 192, 64), 192)], yr, sems("z2"), 0, me.other_core)
    mine = pl.ds(pl.multiple_of(core * 192, 64), 192)

    order = [(b, p) for b in (1, 0) for p in (0, 1)]
    for b, p in order:
        reduce[b, p] = reduce_second(b, p, reduce[b, p])
    z2.wait_recv()
    ts[0] = (yp[0, mine] + yr[0]).astype(BF16)
    ts[1] = (yp[2, mine] + yr[2]).astype(BF16)
    up = send.when(far_high, ts.at[0], tr.at[0], sems("u2h"), (1, 0), me.along(4))
    down = send.when(far_low, ts.at[1], tr.at[1], sems("u2h"), (0, 0), me.along(-4))
    u2_copies = [(far_low, up), (far_high, down)]
    for b, p in order:
        reduce[b, p] = reduce_third(b, p, reduce[b, p])
    for b, p in order:
        reduce[b, p] = reduced(b, p, reduce[b, p])

    halo_arrived(g1_copies)
    for n in (0, 1):
        wide = pl.ds(n * 256, 256)
        total = product(w1_ref[1], g1[:, :, :, wide].reshape(768, 256))
        total = total + (qr[0, :, wide].astype(F32) + qr[1, :, wide].astype(F32))
        slope = gelu_slope(x_ref[:, wide].astype(F32))
        grad_out[:, wide] = (g1[half, core, :, wide].astype(F32) + slope * total).astype(BF16)
    for b, p in order:
        arrived(reduce[b, p])
        reduce[b, p] = gather_second(2 * b + p, p, gh, ge, "e2")
    halo_arrived(u2_copies)
    for m in range(CHUNKS):
        total = yp[1, mine, lanes(m)] + yr[1, :, lanes(m)]
        total = total + (tr[0, :, lanes(m)].astype(F32) + tr[1, :, lanes(m)].astype(F32))
        act_out[:, lanes(m)] = (x1[OWN, :, lanes(m)].astype(F32) + total).astype(BF16)
    for b, p in order:
        arrived(reduce[b, p])
        reduce[b, p] = gather_first(b, p, ge, gf, "e1")

    def unpack(b, out):
        def step(k, _):
            tap, i = lax.div(k, 12), lax.rem(k, 12)
            rows = pl.ds(pl.multiple_of(i * 16, 16), 16)
            for t in range(6):
                out[tap, rows, t * 128 : (t + 1) * 128] = gf[b, k * 6 + t]
            return 0

        lax.fori_loop(0, 36, step, 0)

    for b, out in ((1, far_out), (0, near_out)):
        arrived(reduce[b, 0])
        arrived(reduce[b, 1])
        unpack(b, out)
    send.finish()


def buffers():
    table = {}

    def keep(name, *shape, dtype=BF16):
        table[name] = pltpu.VMEM(shape, dtype)

    def pair(name, *shape):
        table[name + "_s"] = pltpu.SemaphoreType.DMA(shape)
        table[name + "_r"] = pltpu.SemaphoreType.DMA(shape)

    keep("xr", 192, ROWS)
    keep("x1", 2, 192, ROWS)
    keep("u1", 3, 2, 192, ROWS)
    keep("u2", 2, 192, ROWS)
    keep("g2", 3, 2, 2, 192, ROWS)
    keep("g1", 2, 2, 192, ROWS)
    keep("wo1", 3, 192, 768)
    keep("wo2", 3, 192, 768)
    keep("zp", 768, ROWS, dtype=F32)
    keep("zr", 2, 192, ROWS, dtype=F32)
    keep("v", 2, 192, ROWS, dtype=F32)
    keep("yp", 3, 384, ROWS, dtype=F32)
    keep("yr", 3, 192, ROWS, dtype=F32)
    for name in ("qs", "qr", "ts", "tr"):
        keep(name, 2, 192, ROWS)
    keep("wu", 4, 16, 128)
    keep("wh", 4, 8, 16, 128)
    keep("we", 4, 32, 16, 128)
    keep("wf", 2, 216, 16, 128)
    keep("d1", 2, 216, 16, 128)
    keep("r1", 4, 3, UNITS, 16, 128)
    keep("d2", 4, 32, 16, 128)
    keep("r2", 4, 3, 8, 16, 128)
    keep("d3", 4, 8, 16, 128)
    keep("r3", 4, 7, 16, 128)
    keep("gh", 4, 8, 16, 128)
    keep("ge", 4, 32, 16, 128)
    keep("gf", 2, 216, 16, 128)
    pair("wx", 4)
    pair("xx", CHUNKS)
    pair("cx", CHUNKS)
    for name in ("wz", "gz", "s3"):
        pair(name, 4, 7)
    for name in ("w2", "w1", "s1", "s2", "e2", "e1"):
        pair(name, 4, 3)
    for name in ("u1h", "g2h", "g2s"):
        pair(name, 2, CHUNKS + 1)
    pair("u2h", 2, 1)
    pair("g1h", 2, 1)
    pair("g2c", CHUNKS + 1)
    for name in ("g1c", "z1"):
        pair(name, 2)
    pair("z2", 1)
    return table


SCRATCH = buffers()


def body(inputs, cotangent, first_kernel_weight, second_kernel_weight):
    shapes = [jax.ShapeDtypeStruct((192, ROWS), BF16)] * 2 + [jax.ShapeDtypeStruct((3, 192, 768), BF16)] * 2
    vmem = pl.BlockSpec(memory_space=pltpu.VMEM)
    act, grad, near, far = pl.pallas_call(
        kernel,
        out_shape=tuple(shapes),
        in_specs=[vmem] * 4,
        out_specs=(vmem,) * 4,
        scratch_shapes=list(SCRATCH.values()),
        compiler_params=pltpu.CompilerParams(
            collective_id=0, has_side_effects=True, vmem_limit_bytes=56 * 2**20
        ),
    )(inputs.T, cotangent.T, first_kernel_weight, second_kernel_weight)
    return act.T, grad.T, near, far


def solution(mesh):
    return jax.shard_map(
        body,
        mesh=mesh,
        in_specs=(P("bins", "ch"), P("bins", "ch"), P(None, "ch", None), P(None, "ch", None)),
        out_specs=(P("bins", "ch"), P("bins", "ch"), P(None, "ch", None), P(None, "ch", None)),
        check_vma=False,
    )
```

```python
import math

import jax
import jax.numpy as jnp
from jax import lax
from jax.experimental import pallas as pl
from jax.experimental.pallas import tpu as pltpu
from jax.sharding import PartitionSpec as P

MESH = pl.DeviceIdType.MESH
ROWS = 512
CHUNKS = 4
CHUNK = ROWS // CHUNKS
UNITS = 27
WINDOW = 3
LAST_BIN = 127
BINS = 65536
F32, BF16 = jnp.float32, jnp.bfloat16

gelu_coeff = 0.7978845608

AXES = (("x", "y"), ("y", "x"))


def gelu_value(values):
    inner = gelu_coeff * (values + 0.044715 * values * values * values)
    return 0.5 * values * (1.0 + jnp.tanh(inner))


def gelu_slope(values):
    inner = gelu_coeff * (values + 0.044715 * values * values * values)
    tangent = jnp.tanh(inner)
    return 0.5 * (1.0 + tangent) + 0.5 * values * (1.0 - tangent * tangent) * gelu_coeff * (
        1.0 + 3.0 * 0.044715 * values * values
    )


def product(left, right):
    return jnp.dot(left, right, preferred_element_type=F32)


def against(left, right):
    return lax.dot_general(left, right, (((1,), (1,)), ((), ())), preferred_element_type=F32)


def over_rows(left, right):
    return lax.dot_general(left, right, (((0,), (0,)), ((), ())), preferred_element_type=F32)


class Place:
    def __init__(self):
        b = lax.axis_index("bins")
        self.b = b
        self.ch = lax.axis_index("ch")
        self.half = lax.div(self.ch, 2)
        self.core = lax.rem(self.ch, 2)
        self.x = lax.rem(b, 4)
        self.y = lax.rem(lax.div(b, 4), 4)
        self.z = lax.div(b, 16)
        self.other_half = (b, lax.rem(self.ch + 2, 4))
        self.other_core = (b, self.half * 2 + 1 - self.core)

    def shifted(self, axis, d):
        x, y, z = self.x, self.y, self.z
        if axis == "x":
            x = lax.rem(x + d, 4)
        elif axis == "y":
            y = lax.rem(y + d, 4)
        else:
            z = lax.rem(z + d, 8)
        return (z * 16 + y * 4 + x, self.ch)

    def along(self, distance):
        return (lax.rem(self.b + distance + 128, 128), self.ch)

    def coordinate(self, axis):
        return {"x": self.x, "y": self.y, "z": self.z}[axis]


def remote(src, dst, send_sem, recv_sem, target):
    return pltpu.make_async_remote_copy(
        src_ref=src,
        dst_ref=dst,
        send_sem=send_sem,
        recv_sem=recv_sem,
        device_id=target,
        device_id_type=MESH,
    )


class Sender:
    def __init__(self):
        self.pending = []

    def __call__(self, src, dst, sems, index, target):
        copy = remote(src, dst, sems[0].at[index], sems[1].at[index], target)
        copy.start()
        self.pending.append((None, copy))
        return copy

    def when(self, condition, src, dst, sems, index, target):
        copy = remote(src, dst, sems[0].at[index], sems[1].at[index], target)

        @pl.when(condition)
        def _():
            copy.start()

        self.pending.append((condition, copy))
        return copy

    def finish(self):
        for condition, copy in self.pending:
            if condition is None:
                copy.wait_send()
            else:
                pl.when(condition)(copy.wait_send)


def kernel(x_ref, c_ref, w1_hbm, w2_hbm, act_out, grad_out, near_out, far_out, *scratch):
    s = dict(zip(SCRATCH, scratch))
    w1_ref, w2_ref = s["w1v"], s["w2v"]
    loads = [
        pltpu.make_async_copy(src, dst, s["load"].at[k])
        for k, (src, dst) in enumerate(((w1_hbm, w1_ref), (w2_hbm, w2_ref)))
    ]
    for load in loads:
        load.start()
    me = Place()
    half, core = me.half, me.core
    send = Sender()
    barrier = pltpu.get_barrier_semaphore()

    def sems(name):
        return s[name + "_s"], s[name + "_r"], name

    near_low, near_high = me.b >= 1, me.b <= LAST_BIN - 1
    far_low, far_high = me.b >= 4, me.b <= LAST_BIN - 4

    for axis, n in (("x", 4), ("y", 4), ("z", 8)):
        for d in range(1, n):
            pl.semaphore_signal(barrier, inc=1, device_id=me.shifted(axis, d), device_id_type=MESH)
    pl.semaphore_signal(barrier, inc=1, device_id=me.other_half, device_id_type=MESH)
    pl.semaphore_signal(barrier, inc=1, device_id=me.other_core, device_id_type=MESH)
    for hops, condition in ((-1, near_low), (1, near_high), (-4, far_low), (4, far_high)):

        @pl.when(condition)
        def _(hops=hops):
            pl.semaphore_signal(barrier, inc=1, device_id=me.along(hops), device_id_type=MESH)

    xr, u1, x1, u2, g2, g1 = (s[n] for n in ("xr", "u1", "x1", "u2", "g2", "g1"))
    OWN, OTHER = 0, 1

    def own(array, tap):
        return array.at[tap, half, core]

    def other(array, tap):
        return array.at[tap, 1 - half, core]

    def blank(condition, ref):
        @pl.when(jnp.logical_not(condition))
        def _():
            ref[...] = jnp.zeros(ref.shape, ref.dtype)

    blank(near_low, u1.at[0])
    blank(near_high, u1.at[2])
    qs, qr, ts, tr = s["qs"], s["qr"], s["ts"], s["tr"]
    blank(near_high, qr.at[0])
    blank(near_low, qr.at[1])
    blank(far_low, tr.at[0])
    blank(far_high, tr.at[1])
    for h in (0, 1):
        blank(far_high, g2.at[0, h, core])
        blank(far_low, g2.at[2, h, core])

    def lanes(m):
        return pl.ds(m * CHUNK, CHUNK)

    def own_gelu(r, _):
        rows = pl.ds(pl.multiple_of(r * 16, 16), 16)
        u1[1, OWN, rows] = gelu_value(x_ref[rows].astype(F32)).astype(BF16)
        return 0

    lax.fori_loop(0, 12, own_gelu, 0)

    wires = 15 + sum(c.astype(jnp.int32) for c in (near_low, near_high, far_low, far_high))
    pl.semaphore_wait(barrier, wires)

    for load in loads:
        load.wait()
    weights = (w1_ref, w2_ref)
    parts = [(b, p) for b in (0, 1) for p in (0, 1)]

    wh, we, wf = s["wh"], s["we"], s["wf"]
    crossing = {}
    for b, p in parts:
        i = 2 * b + p
        first, second = me.coordinate(AXES[p][0]), me.coordinate(AXES[p][1])
        place = lax.rem(second * 8 + me.z, UNITS)
        unit = p * 108 + first * UNITS + place
        tap = lax.div(unit, 72)
        rest = lax.rem(unit, 72)
        row = pl.multiple_of(lax.div(rest, 6) * 16, 16)
        col = pl.multiple_of(lax.rem(rest, 6) * 128, 128)
        crossing[i] = send(
            weights[b].at[tap, pl.ds(row, 16), pl.ds(col, 128)], s["wu"].at[i], sems("wx"), i, me.other_half
        )

    crossed = []

    def cross():
        n = len(crossed)
        if n >= 2 * CHUNKS:
            return
        m = n % CHUNKS
        if n < CHUNKS:
            crossed.append(send(x_ref.at[:, lanes(m)], xr.at[:, lanes(m)], sems("xx"), m, me.other_half))
        else:
            crossed.append(
                send(c_ref.at[:, lanes(m)], own(g2, 1).at[:, lanes(m)], sems("cx"), m, me.other_half)
            )

    for _ in range(WINDOW):
        cross()

    def halo(low, high, distance, src, low_dst, high_dst, name, index):
        down = send.when(low, src, low_dst, sems(name), (0,) + index, me.along(-distance))
        up = send.when(high, src, high_dst, sems(name), (1,) + index, me.along(distance))
        return [(high, down), (low, up)]

    def halo_arrived(copies):
        for condition, copy in copies:
            pl.when(condition)(copy.wait_recv)

    def arrived(copies):
        for copy in copies:
            copy.wait_recv()

    u1_own = halo(near_low, near_high, 1, u1.at[1, OWN], u1.at[2, OWN], u1.at[0, OWN], "u1h", (CHUNKS,))
    g2_core = [send(c_ref, own(g2, 1), sems("g2c"), CHUNKS, me.other_core)]

    def own_cotangent(r, _):
        rows = pl.ds(pl.multiple_of(r * 16, 16), 16)
        g2[1, half, core, rows] = c_ref[rows]
        return 0

    lax.fori_loop(0, 12, own_cotangent, 0)

    def gather_lines(i, grouped, name):
        return [
            send(grouped.at[i, me.z], grouped.at[i, me.z], sems(name), (i, d - 1), me.shifted("z", d))
            for d in range(1, 8)
        ]

    def gather_second(i, p, grouped, wide, name):
        axis = AXES[p][1]
        there = pl.ds(me.coordinate(axis) * 8, 8)
        copies = [
            send(grouped.at[i], wide.at[i, there], sems(name), (i, d - 1), me.shifted(axis, d)) for d in (1, 2, 3)
        ]
        wide[i, there] = grouped[i]
        return copies

    def gather_first(b, p, wide, whole, name):
        axis = AXES[p][0]
        i = 2 * b + p
        here = pl.ds(p * 108 + me.coordinate(axis) * UNITS, UNITS)
        copies = [
            send(wide.at[i, pl.ds(0, UNITS)], whole.at[b, here], sems(name), (i, d - 1), me.shifted(axis, d))
            for d in (1, 2, 3)
        ]
        whole[b, here] = wide[i, :UNITS]
        return copies

    u1_copies = []

    def x_chunk(m):
        crossed[m].wait_recv()
        cross()
        u1[1, OTHER, :, lanes(m)] = gelu_value(xr[:, lanes(m)].astype(F32)).astype(BF16)
        src = u1.at[1, OTHER, :, lanes(m)]
        u1_copies.extend(
            halo(near_low, near_high, 1, src, u1.at[2, OTHER, :, lanes(m)], u1.at[0, OTHER, :, lanes(m)], "u1h", (m,))
        )

    g2_copies = {}

    def c_chunk(m):
        crossed[CHUNKS + m].wait_recv()
        cross()
        src = other(g2, 1).at[:, lanes(m)]
        g2_copies[m] = halo(
            far_low, far_high, 4, src, other(g2, 0).at[:, lanes(m)], other(g2, 2).at[:, lanes(m)], "g2h", (m,)
        )
        g2_core.append(send(src, src, sems("g2c"), m, me.other_core))

    g2_spread = []

    def g2_forward_own():
        halo_arrived(g2_own)
        for k, tap in enumerate((0, 2)):
            g2_spread.append(send(own(g2, tap), own(g2, tap), sems("g2s"), (k, CHUNKS), me.other_core))

    def g2_forward(m):
        halo_arrived(g2_copies[m])
        for k, tap in enumerate((0, 2)):
            src = other(g2, tap).at[:, lanes(m)]
            g2_spread.append(send(src, src, sems("g2s"), (k, m), me.other_core))

    zp, zr = s["zp"], s["zr"]

    def conv_one(weight, slot, add):
        def step(n, _):
            columns = pl.ds(pl.multiple_of(n * 128, 128), 128)
            rows = pl.ds(pl.multiple_of(n * 128, 128), 128)
            total = over_rows(weight[0, :, columns], u1[0, slot])
            total = total + over_rows(weight[1, :, columns], u1[1, slot])
            total = total + over_rows(weight[2, :, columns], u1[2, slot])
            if add:
                total = total + zp[rows]
            zp[rows] = total
            return 0

        lax.fori_loop(0, 6, step, 0)

    def assemble(b, out):
        def step(k, _):
            tap, i = lax.div(k, 12), lax.rem(k, 12)
            rows = pl.ds(pl.multiple_of(i * 16, 16), 16)
            for t in range(6):
                out[tap, rows, t * 128 : (t + 1) * 128] = wf[b, k * 6 + t]
            return 0

        lax.fori_loop(0, 36, step, 0)

    wo1, wo2 = s["wo1"], s["wo2"]
    lines, seconds, firsts = {}, {}, {}
    for b, p in parts:
        i = 2 * b + p
        crossing[i].wait_recv()
        wh[i, me.z] = s["wu"][i]
        lines[i] = gather_lines(i, wh, "wz")
    x_chunk(0)
    for b, p in parts:
        i = 2 * b + p
        arrived(lines[i])
        seconds[i] = gather_second(i, p, wh, we, "w2")
    x_chunk(1)
    for b, p in parts:
        i = 2 * b + p
        arrived(seconds[i])
        firsts[i] = gather_first(b, p, we, wf, "w1")
    x_chunk(2)
    halo_arrived(u1_own)
    conv_one(w1_ref, OWN, False)
    x_chunk(3)
    g2_own = halo(far_low, far_high, 4, c_ref, own(g2, 0), own(g2, 2), "g2h", (CHUNKS,))
    arrived(firsts[0])
    arrived(firsts[1])
    assemble(0, wo1)
    c_chunk(0)
    halo_arrived(u1_copies)
    conv_one(wo1, OTHER, True)

    def group_rows(h, c):
        return pl.ds(pl.multiple_of((h * 2 + c) * 192, 64), 192)

    z1 = [send(zp.at[group_rows(h, 1 - core)], zr.at[h], sems("z1"), h, me.other_core) for h in (0, 1)]
    c_chunk(1)
    arrived(z1)

    def x1_chunk(m):
        for slot, h in ((OWN, half), (OTHER, 1 - half)):
            before = x_ref[:, lanes(m)] if slot == OWN else xr[:, lanes(m)]
            total = zp[group_rows(h, core), lanes(m)] + zr[h, :, lanes(m)]
            value = (before.astype(F32) + total).astype(BF16)
            x1[slot, :, lanes(m)] = value
            u2[slot, :, lanes(m)] = gelu_value(value.astype(F32)).astype(BF16)

    for m in range(CHUNKS):
        x1_chunk(m)
    arrived(firsts[2])
    arrived(firsts[3])
    assemble(1, wo2)
    g2_forward_own()
    g2_forward(0)
    c_chunk(2)
    g2_forward(1)

    v = s["v"]

    def half_columns(h):
        return pl.ds(pl.multiple_of(h * 384, 128), 384)

    arrived(g2_core[:1])
    arrived(g2_spread[:2])
    for slot, weight in ((OWN, w2_ref), (OTHER, wo2)):
        total = product(weight[0, :, half_columns(half)], g2[0, half].reshape(384, ROWS))
        total = total + product(weight[1, :, half_columns(half)], g2[1, half].reshape(384, ROWS))
        v[slot] = total + product(weight[2, :, half_columns(half)], g2[2, half].reshape(384, ROWS))
    c_chunk(3)
    g2_forward(2)
    g2_forward(3)

    d1, r1, d2, r2, d3, r3 = (s[n] for n in ("d1", "r1", "d2", "r2", "d3", "r3"))

    def weight_grad(b, left, right):
        def step(tap, _):
            for h in (0, 1):
                value = against(left(tap), right(tap, h).reshape(384, ROWS)).astype(BF16)
                for t in range(3):
                    for i in range(12):
                        d1[b, tap * 72 + i * 6 + h * 3 + t] = value[i * 16 : i * 16 + 16, t * 128 : t * 128 + 128]
            return 0

        lax.fori_loop(0, 3, step, 0)

    def reduce_first(b, p):
        i = 2 * b + p
        axis = AXES[p][0]
        here = me.coordinate(axis)
        return [
            send(
                d1.at[b, pl.ds(p * 108 + lax.rem(here + d, 4) * UNITS, UNITS)],
                r1.at[i, d - 1],
                sems("s1"),
                (i, d - 1),
                me.shifted(axis, d),
            )
            for d in (1, 2, 3)
        ]

    def reduce_second(b, p, copies):
        i = 2 * b + p
        arrived(copies)
        base = p * 108 + me.coordinate(AXES[p][0]) * UNITS

        def step(r, _):
            total = d1[b, pl.ds(base + r * 9, 9)].astype(F32)
            for d in range(3):
                total = total + r1[i, d, pl.ds(r * 9, 9)].astype(F32)
            d2[i, pl.ds(r * 9, 9)] = total.astype(BF16)
            return 0

        lax.fori_loop(0, 3, step, 0)
        d2[i, UNITS:] = jnp.zeros((32 - UNITS, 16, 128), BF16)
        axis = AXES[p][1]
        there = me.coordinate(axis)
        return [
            send(
                d2.at[i, pl.ds(lax.rem(there + d, 4) * 8, 8)], r2.at[i, d - 1], sems("s2"), (i, d - 1),
                me.shifted(axis, d),
            )
            for d in (1, 2, 3)
        ]

    def reduce_third(b, p, copies):
        i = 2 * b + p
        arrived(copies)
        there = me.coordinate(AXES[p][1])
        total = d2[i, pl.ds(there * 8, 8)].astype(F32)
        for d in range(3):
            total = total + r2[i, d].astype(F32)
        d3[i] = total.astype(BF16)
        return [
            send(d3.at[i, lax.rem(me.z + d, 8)], r3.at[i, d - 1], sems("s3"), (i, d - 1), me.shifted("z", d))
            for d in range(1, 8)
        ]

    gh, ge, gf = s["gh"], s["ge"], s["gf"]

    def reduced(b, p, copies):
        i = 2 * b + p
        arrived(copies)
        total = d3[i, me.z].astype(F32)
        for d in range(7):
            total = total + r3[i, d].astype(F32)
        gh[i, me.z] = (total * (1.0 / math.sqrt(BINS))).astype(BF16)
        return gather_lines(i, gh, "gz")

    reduce = {}
    arrived(g2_core[1:])
    arrived(g2_spread[2:])
    g1_core = []

    def back_two(n):
        wide = pl.ds(n * 256, 256)
        for slot, weight, h in ((OWN, w2_ref, half), (OTHER, wo2, 1 - half)):
            total = v[slot, :, wide]
            for tap in range(3):
                grad = g2[tap, 1 - half, :, :, wide].reshape(384, 256)
                total = total + product(weight[tap, :, half_columns(1 - half)], grad)
            slope = gelu_slope(x1[slot, :, wide].astype(F32))
            g1[h, core, :, wide] = (g2[1, h, core, :, wide].astype(F32) + slope * total).astype(BF16)
        src = g1.at[:, core, :, wide]
        g1_core.append(send(src, src, sems("g1c"), n, me.other_core))

    weight_grad(1, lambda tap: u2[OWN], lambda tap, h: g2[tap, h])
    for p in (0, 1):
        reduce[1, p] = reduce_first(1, p)
    back_two(0)
    back_two(1)
    arrived(g1_core)
    weight_grad(0, lambda tap: u1[tap, OWN], lambda tap, h: g1[h])
    for p in (0, 1):
        reduce[0, p] = reduce_first(0, p)

    yp, yr = s["yp"], s["yr"]

    def conv_two(n, _):
        columns = pl.ds(pl.multiple_of(half * 384 + n * 128, 128), 128)
        for tap in range(3):
            total = over_rows(w2_ref[tap, :, columns], u2[OWN]) + over_rows(wo2[tap, :, columns], u2[OTHER])
            yp[tap, pl.ds(pl.multiple_of(n * 128, 128), 128)] = total
        return 0

    for k, tap in enumerate((0, 2)):
        qs[k] = product(w1_ref[tap], g1[...].reshape(768, ROWS)).astype(BF16)
    lax.fori_loop(0, 3, conv_two, 0)
    z2 = send(yp.at[:, pl.ds(pl.multiple_of((1 - core) * 192, 64), 192)], yr, sems("z2"), 0, me.other_core)
    mine = pl.ds(pl.multiple_of(core * 192, 64), 192)

    order = [(b, p) for b in (1, 0) for p in (0, 1)]
    for b, p in order:
        reduce[b, p] = reduce_second(b, p, reduce[b, p])
    down = send.when(near_low, qs.at[0], qr.at[0], sems("g1h"), (0, 0), me.along(-1))
    up = send.when(near_high, qs.at[1], qr.at[1], sems("g1h"), (1, 0), me.along(1))
    g1_copies = [(near_high, down), (near_low, up)]
    z2.wait_recv()
    ts[0] = (yp[0, mine] + yr[0]).astype(BF16)
    ts[1] = (yp[2, mine] + yr[2]).astype(BF16)
    up = send.when(far_high, ts.at[0], tr.at[0], sems("u2h"), (1, 0), me.along(4))
    down = send.when(far_low, ts.at[1], tr.at[1], sems("u2h"), (0, 0), me.along(-4))
    u2_copies = [(far_low, up), (far_high, down)]
    for b, p in order:
        reduce[b, p] = reduce_third(b, p, reduce[b, p])
    for b, p in order:
        reduce[b, p] = reduced(b, p, reduce[b, p])

    halo_arrived(g1_copies)
    for n in (0, 1):
        wide = pl.ds(n * 256, 256)
        total = product(w1_ref[1], g1[:, :, :, wide].reshape(768, 256))
        total = total + (qr[0, :, wide].astype(F32) + qr[1, :, wide].astype(F32))
        slope = gelu_slope(x_ref[:, wide].astype(F32))
        grad_out[:, wide] = (g1[half, core, :, wide].astype(F32) + slope * total).astype(BF16)
    for b, p in order:
        arrived(reduce[b, p])
        reduce[b, p] = gather_second(2 * b + p, p, gh, ge, "e2")
    halo_arrived(u2_copies)
    for m in range(CHUNKS):
        total = yp[1, mine, lanes(m)] + yr[1, :, lanes(m)]
        total = total + (tr[0, :, lanes(m)].astype(F32) + tr[1, :, lanes(m)].astype(F32))
        act_out[:, lanes(m)] = (x1[OWN, :, lanes(m)].astype(F32) + total).astype(BF16)
    for b, p in order:
        arrived(reduce[b, p])
        reduce[b, p] = gather_first(b, p, ge, gf, "e1")

    def unpack(b, out):
        def step(k, _):
            tap, i = lax.div(k, 12), lax.rem(k, 12)
            rows = pl.ds(pl.multiple_of(i * 16, 16), 16)
            for t in range(6):
                out[tap, rows, t * 128 : (t + 1) * 128] = gf[b, k * 6 + t]
            return 0

        lax.fori_loop(0, 36, step, 0)

    for b, out in ((1, far_out), (0, near_out)):
        arrived(reduce[b, 0])
        arrived(reduce[b, 1])
        unpack(b, out)
    send.finish()


def buffers():
    table = {}

    def keep(name, *shape, dtype=BF16):
        table[name] = pltpu.VMEM(shape, dtype)

    def pair(name, *shape):
        table[name + "_s"] = pltpu.SemaphoreType.DMA(shape)
        table[name + "_r"] = pltpu.SemaphoreType.DMA(shape)

    keep("xr", 192, ROWS)
    keep("w1v", 3, 192, 768)
    keep("w2v", 3, 192, 768)
    table["load"] = pltpu.SemaphoreType.DMA((2,))
    keep("x1", 2, 192, ROWS)
    keep("u1", 3, 2, 192, ROWS)
    keep("u2", 2, 192, ROWS)
    keep("g2", 3, 2, 2, 192, ROWS)
    keep("g1", 2, 2, 192, ROWS)
    keep("wo1", 3, 192, 768)
    keep("wo2", 3, 192, 768)
    keep("zp", 768, ROWS, dtype=F32)
    keep("zr", 2, 192, ROWS, dtype=F32)
    keep("v", 2, 192, ROWS, dtype=F32)
    keep("yp", 3, 384, ROWS, dtype=F32)
    keep("yr", 3, 192, ROWS, dtype=F32)
    for name in ("qs", "qr", "ts", "tr"):
        keep(name, 2, 192, ROWS)
    keep("wu", 4, 16, 128)
    keep("wh", 4, 8, 16, 128)
    keep("we", 4, 32, 16, 128)
    keep("wf", 2, 216, 16, 128)
    keep("d1", 2, 216, 16, 128)
    keep("r1", 4, 3, UNITS, 16, 128)
    keep("d2", 4, 32, 16, 128)
    keep("r2", 4, 3, 8, 16, 128)
    keep("d3", 4, 8, 16, 128)
    keep("r3", 4, 7, 16, 128)
    keep("gh", 4, 8, 16, 128)
    keep("ge", 4, 32, 16, 128)
    keep("gf", 2, 216, 16, 128)
    pair("wx", 4)
    pair("xx", CHUNKS)
    pair("cx", CHUNKS)
    for name in ("wz", "gz", "s3"):
        pair(name, 4, 7)
    for name in ("w2", "w1", "s1", "s2", "e2", "e1"):
        pair(name, 4, 3)
    for name in ("u1h", "g2h", "g2s"):
        pair(name, 2, CHUNKS + 1)
    pair("u2h", 2, 1)
    pair("g1h", 2, 1)
    pair("g2c", CHUNKS + 1)
    for name in ("g1c", "z1"):
        pair(name, 2)
    pair("z2", 1)
    return table


SCRATCH = buffers()


def body(inputs, cotangent, first_kernel_weight, second_kernel_weight):
    shapes = [jax.ShapeDtypeStruct((192, ROWS), BF16)] * 2 + [jax.ShapeDtypeStruct((3, 192, 768), BF16)] * 2
    vmem = pl.BlockSpec(memory_space=pltpu.VMEM)
    act, grad, near, far = pl.pallas_call(
        kernel,
        out_shape=tuple(shapes),
        in_specs=[vmem] * 2 + [pl.BlockSpec(memory_space=pl.ANY)] * 2,
        out_specs=(vmem,) * 4,
        scratch_shapes=list(SCRATCH.values()),
        compiler_params=pltpu.CompilerParams(
            collective_id=0, has_side_effects=True, vmem_limit_bytes=56 * 2**20
        ),
    )(inputs.T, cotangent.T, first_kernel_weight, second_kernel_weight)
    return act.T, grad.T, near, far


def solution(mesh):
    return jax.shard_map(
        body,
        mesh=mesh,
        in_specs=(P("bins", "ch"), P("bins", "ch"), P(None, "ch", None), P(None, "ch", None)),
        out_specs=(P("bins", "ch"), P("bins", "ch"), P(None, "ch", None), P(None, "ch", None)),
        check_vma=False,
    )
```
